32 devices in a mesh: wide: 8 (over z, x), narrow: 4 (over y, core).
Axes of the slice: x: 2, y: 2, z: 4, core: 2. Of those that a mesh axis runs over, the one named last changes fastest.
Arguments:
- a_blocks: bfloat16 [32, 8, 2, 128, 128], P('wide', 'narrow'), may hold values from -0.125 to 0.125
- a_cols: int32 [32, 8, 2], P('wide'), may hold values from 0 to 1
- a_scales: float32 [32, 8, 2], P('wide'), may hold values from 0.3 to 3
- a_counts: int32 [32, 8], P('wide'), may hold values from 0 to 2
- b_panel: bfloat16 [2048, 1024], P('wide', 'narrow'), may hold values from -6 to 6
- b_scales: float32 [16], replicated, may hold values from 0.3 to 3
- keep_mask: int32 [32, 8], P('wide', 'narrow'), may hold values 0 or 1
- row_perm: int32 [8, 4], P('wide'), may hold values from 0 to 3, each once within a row
Outputs:
- relaid: bfloat16 [4096, 1024], P(('wide', 'narrow'))
The draws below stay inside these ranges and needn't reach their ends.
Inputs may be any that keep to these rules, and one draw needn't show every extreme that they name: `a_counts`: slots at or beyond the count hold no block of the operand. `row_perm`: each row holds every number from 0 to 3 once.
All inputs are finite; a program needn't handle non-finite values. No bound on the sum of `keep_mask` on one device may be relied on, other than what follows from the above.
Results may differ from the reference program's by a relative error of at most 0.0049.
Values may be sent and summed in bfloat16 or wider, within the bound.
A program may use at most 64 MiB of HBM per device.

```python
import math
import jax
import jax.numpy as jnp
from jax import lax

BLK = 128
BR = 4
KB = 2
SA = 2
SECTIONS = 8
NRB = 32
NKB = 16
NCB = 8
GROUPS = 8
N_WIDE = 8


def set_ends(array, rng, least, high):
    extent = array.shape
    spot = [jax.random.randint(jax.random.fold_in(rng, axis), (), 0, extent[axis]) for axis in range(len(extent))]
    array = array.at[tuple(spot)].set(least)
    longest = extent.index(max(extent))
    spot[longest] = (spot[longest] + 1) % extent[longest]
    return array.at[tuple(spot)].set(high)


def level_of(rng, shape, shards, low, top_value):
    loudness, own = 1.0, jax.random.fold_in(rng, 6)
    for dim, parts in shards:
        draws = jnp.exp(jax.random.uniform(jax.random.fold_in(own, dim), (parts,), jnp.float32, low / len(shards), top_value / len(shards)))
        loudness = loudness * jnp.repeat(draws, shape[dim] // parts).reshape([-1 if axis == dim else 1 for axis in range(len(shape))])
    return loudness


def gaussian(own_key, dims, scale, bound, pieces=(), kind=jnp.bfloat16):
    drawn = jax.random.normal(own_key, dims, jnp.float32) * scale
    if len(pieces) > 0:
        drawn = level_of(own_key, dims, pieces, -0.22, 0.18) * drawn
    return jnp.clip(drawn, min=-bound, max=bound).astype(kind)


def setup_inputs(seed: int = 0) -> dict:
    splits = jax.random.split(jax.random.key(seed), 9)
    a_blocks = gaussian(splits[0], (NRB, SECTIONS, SA, BLK, BLK), (BLK * SA * SECTIONS) ** -0.5, 0.125, ((0, 8), (1, 4)))
    a_cols = set_ends(jax.random.randint(splits[1], (NRB, SECTIONS, SA), 0, KB), jax.random.fold_in(splits[1], 1), 0, KB - 1).astype(jnp.int32)
    a_scales = jnp.clip(jnp.exp(math.log(3.0) - 2.3025851 * jax.random.uniform(splits[2], (NRB, SECTIONS, SA), jnp.float32) ** level_of(splits[2], (NRB, SECTIONS, SA), ((0, 8),), -0.2, 0.2)), 0.3, 3.0)
    a_counts = set_ends(jax.random.randint(splits[3], (NRB, SECTIONS), 0, SA + 1), jax.random.fold_in(splits[3], 1), 0, SA).astype(jnp.int32)
    b_panel = gaussian(splits[4], (NKB * BLK, NCB * BLK), 1.0, 6.0, ((0, 8), (1, 4)))
    b_scales = jnp.clip(jnp.exp(jax.random.uniform(splits[5], (NKB,), jnp.float32, math.log(0.3), math.log(3.0))), 0.3, 3.0)
    keep_mask = set_ends((jax.random.randint(splits[6], (NRB, NCB), 0, 4) < 3).astype(jnp.int32), jax.random.fold_in(splits[6], 1), 0, 1)
    row_perm = jax.vmap(lambda own: jax.random.permutation(own, BR))(jax.random.split(splits[7], GROUPS)).reshape((GROUPS, BR)).astype(jnp.int32)
    return dict(a_blocks=a_blocks, a_cols=a_cols, a_scales=a_scales, a_counts=a_counts, b_panel=b_panel, b_scales=b_scales, keep_mask=keep_mask, row_perm=row_perm)


def reference(a_blocks, a_cols, a_scales, a_counts, b_panel, b_scales, keep_mask, row_perm):
    row_total = a_blocks.shape[0]
    block_side = a_blocks.shape[3]
    out_width = b_panel.shape[1]
    col_blocks = out_width // block_side
    b_tiles = b_panel.reshape(-1, block_side, out_width)
    group_of = jnp.arange(row_total, dtype=jnp.int32) // BR
    step_ids = jnp.arange(SECTIONS, dtype=jnp.int32)
    panel_of = (group_of[:, None] - step_ids[None, :]) % N_WIDE
    k_index = (panel_of[:, :, None] * KB + a_cols).astype(jnp.int32)
    live_slots = (jnp.arange(SA, dtype=jnp.int32)[None, None, :] < a_counts[:, :, None]).astype(jnp.float32)
    weights = a_scales * jnp.take(b_scales, k_index) * live_slots

    def one_row(packed):
        row_blocks, row_k, row_weights, row_keep = packed
        scaled = (row_blocks.astype(jnp.float32) * row_weights[:, :, None, None]).astype(jnp.bfloat16)
        left = jnp.transpose(scaled, (2, 0, 1, 3)).reshape(block_side, -1)
        right = jnp.take(b_tiles, row_k.reshape(-1), axis=0).reshape(-1, out_width)
        product = jnp.dot(left, right, preferred_element_type=jnp.float32)
        kept = product.reshape(block_side, col_blocks, block_side) * row_keep.astype(jnp.float32)[None, :, None]
        return kept.astype(jnp.bfloat16).reshape(block_side, out_width)

    filtered = lax.map(one_row, (a_blocks, k_index, weights, keep_mask))
    grouped = filtered.reshape(N_WIDE, BR, block_side, out_width)
    positions = jnp.arange(BR, dtype=jnp.int32)
    matches = (row_perm[:, None, :] == positions[None, :, None]).astype(jnp.int32)
    inverse = jnp.sum(positions[None, None, :] * matches, axis=2).astype(jnp.int32)
    relaid = jnp.take_along_axis(grouped, inverse[:, :, None, None], axis=1)
    return relaid.reshape(row_total * block_side, out_width)
```

```python
import functools

import jax
import jax.numpy as jnp
from jax import lax
from jax.experimental import pallas as pl
from jax.experimental.pallas import tpu as pltpu
from jax.sharding import PartitionSpec as P

MESH = pl.DeviceIdType.MESH
HALVES = 2


def kernel(
    wide_count,
    a_hbm,
    cols_hbm,
    scales_hbm,
    counts_hbm,
    b_hbm,
    b_scales_hbm,
    keep_hbm,
    perm_hbm,
    out,
    cols,
    scales,
    counts,
    b_scales,
    keep,
    perm,
    table_sem,
    a_own,
    left,
    right,
    result,
    partial,
    load_sem,
    b_recv,
    b_up,
    b_down,
    b_cross,
    a_recv,
    a_mate,
    a_far,
    r_send,
    r_recv,
):
    w = lax.axis_index("wide")
    n = lax.axis_index("narrow")
    x = w % 2
    z = w // 2
    depth = wide_count // 2
    rows, share, slots, side = a_own.shape[:4]
    kb = b_hbm.shape[0] // side
    width = b_hbm.shape[1]
    part = b_hbm.shape[0] // HALVES
    across = w + 1 - 2 * x
    mate = n + 1 - 2 * (n % 2)
    far = (n + 2) % 4
    diagonal = 3 - n

    tables = [
        pltpu.make_async_copy(source, kept, table_sem.at[i])
        for i, (source, kept) in enumerate(
            (
                (perm_hbm, perm),
                (cols_hbm, cols),
                (scales_hbm, scales),
                (counts_hbm, counts),
                (b_scales_hbm, b_scales),
                (keep_hbm, keep),
            )
        )
    ]
    for copy in tables:
        copy.start()
    load_a = pltpu.make_async_copy(a_hbm, a_own, load_sem.at[0])
    load_a.start()
    load_b = [
        pltpu.make_async_copy(
            b_hbm.at[pl.ds(h * part, part)], right.at[w * HALVES + h], load_sem.at[1 + h]
        )
        for h in range(HALVES)
    ]
    for copy in load_b:
        copy.start()

    barrier = pltpu.get_barrier_semaphore()
    for peer in ((w, mate), (w, far), (w, diagonal), (across, n)):
        pl.semaphore_signal(barrier, inc=1, device_id=peer, device_id_type=MESH)

    @pl.when(z > 0)
    def _():
        pl.semaphore_signal(barrier, inc=1, device_id=(w - 2, n), device_id_type=MESH)

    @pl.when(z < depth - 1)
    def _():
        pl.semaphore_signal(barrier, inc=1, device_id=(w + 2, n), device_id_type=MESH)

    neighbours = jnp.where(z > 0, 1, 0) + jnp.where(z < depth - 1, 1, 0)
    pl.semaphore_wait(barrier, 4 + neighbours)

    def piece(source, slot, sent, target):
        return pltpu.make_async_remote_copy(
            src_ref=source,
            dst_ref=right.at[slot],
            send_sem=sent.at[slot],
            recv_sem=b_recv.at[slot],
            device_id=(target, n),
            device_id_type=MESH,
        )

    def upward(slot, source=None):
        return piece(right.at[slot] if source is None else source, slot, b_up, w + 2)

    def downward(slot, source=None):
        return piece(right.at[slot] if source is None else source, slot, b_down, w - 2)

    def crossing(slot, source=None):
        return piece(right.at[slot] if source is None else source, slot, b_cross, across)

    for h in range(HALVES):
        own = w * HALVES + h
        source = b_hbm.at[pl.ds(h * part, part)]

        @pl.when(z < depth - 1)
        def _():
            upward(own, source).start()

        @pl.when(z > 0)
        def _():
            downward(own, source).start()

        crossing(own, source).start()

    def block(origin, q, sent, target):
        return pltpu.make_async_remote_copy(
            src_ref=left.at[origin, q],
            dst_ref=left.at[origin, q],
            send_sem=sent,
            recv_sem=a_recv.at[origin, q],
            device_id=(w, target),
            device_id_type=MESH,
        )

    def home(q):
        total = jnp.int32(0)
        for r in range(rows):
            total = jnp.where(perm[0, r] == q, r, total)
        return total

    for copy in tables:
        copy.wait()
    load_a.wait()
    sent_order = (n, mate, diagonal, far)
    for q in sent_order:
        r = home(q)
        for j in range(share):
            s = n * share + j
            panel = (w - s + wide_count) % wide_count
            weights, places = [], []
            for m in range(slots):
                place = cols[r, m, s]
                live = jnp.where(m < counts[r, s], 1.0, 0.0)
                weights.append(scales[r, m, s] * b_scales[panel * kb + place] * live)
                places.append(place)
            for k in range(kb):
                total = None
                for m in range(slots):
                    weight = jnp.where(places[m] == k, weights[m], 0.0)
                    term = a_own[r, j, m].astype(jnp.float32) * weight
                    total = term if total is None else total + term
                left[n, q, j, :, k * side : (k + 1) * side] = total.astype(jnp.bfloat16)
        block(n, q, a_far.at[q], far).start()
        block(n, q, a_mate.at[0, q], mate).start()

    for step in range(1, max(depth, rows + 1)):
        if step < depth:
            for h in range(HALVES):
                from_below = (w - 2 * step) * HALVES + h
                from_above = (w + 2 * step) * HALVES + h

                @pl.when(z - step >= 0)
                def _():
                    upward(from_below).wait_recv()

                    @pl.when(z < depth - 1)
                    def _():
                        upward(from_below).start()

                    crossing(from_below).start()

                @pl.when(z + step < depth)
                def _():
                    downward(from_above).wait_recv()

                    @pl.when(z > 0)
                    def _():
                        downward(from_above).start()

                    crossing(from_above).start()

        if step <= rows:
            q = (far, diagonal, mate, n)[step - 1]
            block(far, q, a_far.at[q], far).wait_recv()
            block(far, q, a_mate.at[1, q], mate).start()

    for copy in load_b:
        copy.wait()
    for q in (far, diagonal, mate, n):
        block(mate, q, a_mate.at[0, q], mate).wait_recv()
    for q in (far, diagonal, mate, n):
        block(diagonal, q, a_mate.at[1, q], mate).wait_recv()

    def panel_product(panel, rows_left):
        s = (w - panel + wide_count) % wide_count
        tile = right[pl.ds(panel * HALVES, HALVES)].reshape(kb * side, width)
        return jnp.dot(rows_left(s // share, s % share), tile, preferred_element_type=jnp.float32)

    for level in range(depth):
        product = panel_product(
            2 * level + x, lambda o, j: left[o, :, j].reshape(rows * side, kb * side)
        ).reshape(rows, side, width)
        partial[...] = product if level == 0 else partial[...] + product
    lower = z < depth // 2
    levels = []
    for turn in range(depth):
        levels.append(jnp.where(lower, turn, depth - 1 - turn))
    near = jnp.where((z == 0) | (z == depth - 1), 0, 1)
    levels[0], levels[1] = (
        jnp.where(near == 0, levels[0], levels[1]),
        jnp.where(near == 0, levels[1], levels[0]),
    )

    def peer_arrived(level):
        for h in range(HALVES):
            crossing((2 * level + 1 - x) * HALVES + h).wait_recv()

    for level in levels[:-1]:
        peer_arrived(level)
        partial[...] = partial[...] + panel_product(
            2 * level + 1 - x, lambda o, j: left[o, :, j].reshape(rows * side, kb * side)
        ).reshape(rows, side, width)
    peer_arrived(levels[-1])

    columns = pl.ds(pl.multiple_of(n * width, width), width)

    def deliver(q):
        return pltpu.make_async_remote_copy(
            src_ref=result.at[q],
            dst_ref=out.at[:, columns],
            send_sem=r_send.at[q],
            recv_sem=r_recv.at[n],
            device_id=(w, q),
            device_id_type=MESH,
        )

    for q in (far, diagonal, mate, n):
        total = partial[q] + panel_product(
            2 * levels[-1] + 1 - x, lambda o, j: left[o, q, j]
        )
        r = home(q)
        kept = []
        for c in range(width // side):
            kept.append(
                total[:, c * side : (c + 1) * side] * keep[c, r].astype(jnp.float32)
            )
        filtered = jnp.concatenate(kept, axis=1).astype(jnp.bfloat16)
        if q is n:
            out[:, columns] = filtered
        else:
            result[q] = filtered
            deliver(q).start()

    for q in (far, diagonal, mate):
        deliver(q).wait_send()
    for q in sent_order:
        block(n, q, a_far.at[q], far).wait_send()
        block(n, q, a_mate.at[0, q], mate).wait_send()
        block(far, q, a_mate.at[1, q], mate).wait_send()
    for h in range(HALVES):
        for step in range(depth):
            from_below = (w - 2 * step) * HALVES + h
            from_above = (w + 2 * step) * HALVES + h

            @pl.when(z - step >= 0)
            def _():
                @pl.when(z < depth - 1)
                def _():
                    upward(from_below).wait_send()

                crossing(from_below).wait_send()

            @pl.when((z + step < depth) & (z > 0))
            def _():
                downward(from_above).wait_send()

            if step > 0:

                @pl.when(z + step < depth)
                def _():
                    crossing(from_above).wait_send()

    for origin in (mate, far, diagonal):
        source_columns = pl.ds(pl.multiple_of(origin * width, width), width)
        pltpu.make_async_remote_copy(
            src_ref=result.at[origin],
            dst_ref=out.at[:, source_columns],
            send_sem=r_send.at[origin],
            recv_sem=r_recv.at[origin],
            device_id=(w, origin),
            device_id_type=MESH,
        ).wait_recv()


def fused(wide_count, a_blocks, a_cols, a_scales, a_counts, b_panel, b_scales, keep_mask, row_perm):
    rows, share, slots, side = a_blocks.shape[:4]
    depth, width = b_panel.shape
    narrow_count = 4
    pieces = wide_count * HALVES
    in_place = pl.BlockSpec(memory_space=pltpu.HBM)
    dma = pltpu.SemaphoreType.DMA
    return pl.pallas_call(
        functools.partial(kernel, wide_count),
        out_shape=pltpu.VMEM((side, width * narrow_count), jnp.bfloat16),
        in_specs=[in_place] * 8,
        out_specs=pl.BlockSpec(memory_space=pltpu.VMEM),
        scratch_shapes=[
            pltpu.SMEM((rows, slots, a_cols.shape[1]), jnp.int32),
            pltpu.SMEM((rows, slots, a_cols.shape[1]), jnp.float32),
            pltpu.SMEM(a_counts.shape, jnp.int32),
            pltpu.SMEM(b_scales.shape, jnp.float32),
            pltpu.SMEM((keep_mask.shape[1], rows), jnp.int32),
            pltpu.SMEM(row_perm.shape, jnp.int32),
            dma((6,)),
            pltpu.VMEM(a_blocks.shape, jnp.bfloat16),
            pltpu.VMEM((narrow_count, rows, share, side, depth), jnp.bfloat16),
            pltpu.VMEM((pieces, depth // HALVES, width), jnp.bfloat16),
            pltpu.VMEM((narrow_count, side, width), jnp.bfloat16),
            pltpu.VMEM((rows, side, width), jnp.float32),
            dma((1 + HALVES,)),
            dma((pieces,)),
            dma((pieces,)),
            dma((pieces,)),
            dma((pieces,)),
            dma((narrow_count, rows)),
            dma((2, rows)),
            dma((rows,)),
            dma((narrow_count,)),
            dma((narrow_count,)),
        ],
        compiler_params=pltpu.CompilerParams(
            collective_id=0, has_side_effects=True, vmem_limit_bytes=60 * 2**20
        ),
    )(
        a_blocks,
        jnp.transpose(a_cols, (0, 2, 1)),
        jnp.transpose(a_scales, (0, 2, 1)),
        a_counts,
        b_panel,
        b_scales,
        jnp.transpose(keep_mask),
        row_perm,
    )


def shifted(block, axis, distance):
    devices = range(lax.axis_size(axis))
    route = [((i - distance) % len(devices), i) for i in devices]
    return lax.ppermute(block, axis, route)


def chosen(table, index):
    tail = (1,) * (table.ndim - 1)
    index = index.reshape(index.shape + tail)
    found = jnp.broadcast_to(table[0], index.shape[: index.ndim - len(tail)] + table.shape[1:])
    for k in range(1, table.shape[0]):
        found = jnp.where(index == k, table[k], found)
    return found


def section_term(row_blocks, slot_cols, weights, b_tiles):
    row_count = row_blocks.shape[0]
    slot_count = row_blocks.shape[1]
    block_side = row_blocks.shape[2]
    scaled = (row_blocks.astype(jnp.float32) * weights[:, :, None, None]).astype(jnp.bfloat16)
    left = jnp.transpose(scaled, (0, 2, 1, 3)).reshape(
        row_count, block_side, slot_count * block_side
    )
    right = chosen(b_tiles, slot_cols.reshape(-1)).reshape(
        row_count, slot_count * block_side, b_tiles.shape[2]
    )
    return jnp.einsum("rik,rkj->rij", left, right, preferred_element_type=jnp.float32)


def by_rings(a_blocks, a_cols, a_scales, a_counts, b_panel, b_scales, keep_mask, row_perm):
    wide_count = lax.axis_size("wide")
    narrow_count = lax.axis_size("narrow")
    device_row = lax.axis_index("wide")
    device_column = lax.axis_index("narrow")
    row_count, section_share, slot_count, block_side = a_blocks.shape[:4]
    section_total = section_share * narrow_count
    k_rows = b_panel.shape[0] // block_side
    out_width = b_panel.shape[1]
    col_blocks = out_width // block_side
    held = [a_blocks]
    for _ in range(narrow_count - 1):
        held.append(shifted(held[-1], "narrow", 1))
    held = jnp.stack(held)
    slot_ids = jnp.arange(slot_count, dtype=jnp.int32)
    accumulated = jnp.zeros((row_count, block_side, out_width), jnp.float32)
    current = b_panel.reshape(k_rows, block_side, out_width)
    for step_number in range(section_total):
        if step_number > 0:
            current = shifted(current, "wide", 1)
        back = (device_column - step_number // section_share) % narrow_count
        row_blocks = lax.dynamic_index_in_dim(held, back, keepdims=False)
        row_blocks = row_blocks[:, step_number % section_share]
        panel_number = (device_row - step_number) % wide_count
        slot_cols = a_cols[:, step_number]
        live_slots = (slot_ids[None, :] < a_counts[:, step_number][:, None]).astype(jnp.float32)
        weights = (
            a_scales[:, step_number]
            * chosen(lax.dynamic_slice(b_scales, (panel_number * k_rows,), (k_rows,)), slot_cols)
            * live_slots
        )
        accumulated = accumulated + section_term(row_blocks, slot_cols, weights, current)
    masked = (
        accumulated.reshape(row_count, block_side, col_blocks, block_side)
        * keep_mask.astype(jnp.float32)[:, None, :, None]
    )
    filtered = masked.astype(jnp.bfloat16).reshape(row_count, block_side, out_width)
    new_order = row_perm[0]
    positions = jnp.arange(row_count, dtype=jnp.int32)
    matches = (new_order[None, :] == positions[:, None]).astype(jnp.int32)
    inverse = jnp.sum(positions[None, :] * matches, axis=1)
    reordered = chosen(filtered, inverse).reshape(row_count * block_side, out_width)
    return lax.all_to_all(reordered, "narrow", split_axis=0, concat_axis=1, tiled=True)


def per_device(*operands):
    wide_count = lax.axis_size("wide")
    narrow_count = lax.axis_size("narrow")
    rows, share = operands[0].shape[:2]
    if narrow_count == 4 and rows == 4 and wide_count == share * narrow_count == 8:
        return fused(wide_count, *operands)
    return by_rings(*operands)


def solution(mesh):
    in_specs = (
        P("wide", "narrow", None, None, None),
        P("wide", None, None),
        P("wide", None, None),
        P("wide", None),
        P("wide", "narrow"),
        P(),
        P("wide", "narrow"),
        P("wide", None),
    )
    out_specs = P(("wide", "narrow"), None)
    return jax.shard_map(
        per_device, mesh=mesh, in_specs=in_specs, out_specs=out_specs, check_vma=False
    )
```

```python
import functools

import jax
import jax.numpy as jnp
from jax import lax
from jax.experimental import pallas as pl
from jax.experimental.pallas import tpu as pltpu
from jax.sharding import PartitionSpec as P

MESH = pl.DeviceIdType.MESH
HALVES = 2
PARTS = 4
WIDE = 8
DEPTH = 4
NARROW = 4
EARLY = 1


def kernel(
    a_hbm,
    cols_hbm,
    scales_hbm,
    counts_hbm,
    b_hbm,
    b_scales_hbm,
    keep_hbm,
    perm_hbm,
    out,
    cols,
    scales,
    counts,
    b_scales,
    keep,
    perm,
    table_sem,
    a_own,
    left,
    right,
    result,
    total,
    load_sem,
    b_recv,
    b_up,
    b_down,
    b_cross,
    a_recv,
    a_mate,
    a_far,
    r_send,
    r_recv,
):
    w = lax.axis_index("wide")
    n = lax.axis_index("narrow")
    x = w % 2
    z = w // 2
    y = n // 2
    core = n % 2
    rows, share, slots, side = a_own.shape[:4]
    kb = b_hbm.shape[0] // side
    width = b_hbm.shape[1]
    across = w + 1 - 2 * x
    mate = n + 1 - 2 * core
    far = (n + 2) % 4
    diagonal = 3 - n

    barrier = pltpu.get_barrier_semaphore()
    for peer in ((w, mate), (w, far), (w, diagonal), (across, n)):
        pl.semaphore_signal(barrier, inc=1, device_id=peer, device_id_type=MESH)

    @pl.when(z > 0)
    def _():
        pl.semaphore_signal(barrier, inc=1, device_id=(w - 2, n), device_id_type=MESH)

    @pl.when(z < DEPTH - 1)
    def _():
        pl.semaphore_signal(barrier, inc=1, device_id=(w + 2, n), device_id_type=MESH)

    tables = [
        pltpu.make_async_copy(source, kept, table_sem.at[i])
        for i, (source, kept) in enumerate(
            (
                (perm_hbm, perm),
                (cols_hbm, cols),
                (scales_hbm, scales),
                (counts_hbm, counts),
                (b_scales_hbm, b_scales),
                (keep_hbm, keep),
            )
        )
    ]
    for copy in tables:
        copy.start()
    load_a = pltpu.make_async_copy(a_hbm, a_own, load_sem.at[0])
    load_a.start()
    load_b = [
        pltpu.make_async_copy(
            b_hbm.at[t % kb * side : (t % kb + 1) * side, t // kb * side : (t // kb + 1) * side],
            right.at[w * PARTS + t],
            load_sem.at[1 + t],
        )
        for t in range(PARTS)
    ]
    for copy in load_b:
        copy.start()

    def piece(slot, sent, target):
        return pltpu.make_async_remote_copy(
            src_ref=right.at[slot],
            dst_ref=right.at[slot],
            send_sem=sent.at[slot],
            recv_sem=b_recv.at[slot],
            device_id=(target, n),
            device_id_type=MESH,
        )

    def upward(slot):
        return piece(slot, b_up, w + 2)

    def downward(slot):
        return piece(slot, b_down, w - 2)

    def crossing(slot):
        return piece(slot, b_cross, across)

    def block(origin, pair, j, sent, target):
        return pltpu.make_async_remote_copy(
            src_ref=left.at[origin, pair, j],
            dst_ref=left.at[origin, pair, j],
            send_sem=sent,
            recv_sem=a_recv.at[origin, pair, j],
            device_id=(w, target),
            device_id_type=MESH,
        )

    def to_far(pair, j):
        return block(n, pair, j, a_far.at[pair, j], far)

    def to_mate(pair, j):
        return block(n, pair, j, a_mate.at[0, pair, j], mate)

    def from_far(pair, j):
        return block(far, pair, j, a_far.at[pair, j], far)

    def pass_on(pair, j):
        return block(far, pair, j, a_mate.at[1, pair, j], mate)

    def home(q):
        found = jnp.int32(0)
        for r in range(rows):
            found = jnp.where(perm[0, r] == q, r, found)
        return found

    def scale(pair, j):
        s = n * share + j
        panel = (w - s + WIDE) % WIDE
        for c in range(2):
            r = home(2 * pair + c)
            weights, places = [], []
            for m in range(slots):
                place = cols[r, m, s]
                live = jnp.where(m < counts[r, s], 1.0, 0.0)
                weights.append(scales[r, m, s] * b_scales[panel * kb + place] * live)
                places.append(place)
            for k in range(kb):
                value = None
                for m in range(slots):
                    weight = jnp.where(places[m] == k, weights[m], 0.0)
                    term = a_own[r, j, m].astype(jnp.float32) * weight
                    value = term if value is None else value + term
                left[n, pair, j, c * side : (c + 1) * side, k * side : (k + 1) * side] = (
                    value.astype(jnp.bfloat16)
                )

    pairs = (y, 1 - y)
    units = [(pair, j) for pair in pairs for j in range(share)]
    for copy in tables:
        copy.wait()
    load_a.wait()
    for unit in units[:EARLY]:
        scale(*unit)
    for copy in load_b:
        copy.wait()

    neighbours = jnp.where(z > 0, 1, 0) + jnp.where(z < DEPTH - 1, 1, 0)
    pl.semaphore_wait(barrier, 4 + neighbours)

    for unit in units[:EARLY]:
        to_far(*unit).start()
    for t in range(PARTS):
        own = w * PARTS + t
        crossing(own).start()

        @pl.when(z < DEPTH - 1)
        def _():
            upward(own).start()

        @pl.when(z > 0)
        def _():
            downward(own).start()

    for unit in units[:EARLY]:
        to_mate(*unit).start()
    for unit in units[EARLY:]:
        scale(*unit)
        to_far(*unit).start()
        to_mate(*unit).start()

    def relay(step, t):
        from_below = (w - 2 * step) * PARTS + t
        from_above = (w + 2 * step) * PARTS + t

        @pl.when(z - step >= 0)
        def _():
            upward(from_below).wait_recv()

            @pl.when(z < DEPTH - 1)
            def _():
                upward(from_below).start()

            crossing(from_below).start()

        @pl.when(z + step < DEPTH)
        def _():
            downward(from_above).wait_recv()

            @pl.when(z > 0)
            def _():
                downward(from_above).start()

            crossing(from_above).start()

    def hand_over(pair, j):
        from_far(pair, j).wait_recv()
        pass_on(pair, j).start()

    def mate_arrived(pair, j):
        block(mate, pair, j, a_mate.at[0, pair, j], mate).wait_recv()

    def diagonal_arrived(pair, j):
        block(diagonal, pair, j, a_mate.at[1, pair, j], mate).wait_recv()

    near = (
        z,
        jnp.where(z == 0, 1, z - 1),
        jnp.where(z == 0, 2, jnp.where(z == 3, 1, z + 1)),
        jnp.where(z < 2, 3, 0),
    )

    def peer_arrived(level, h):
        for t in range(h * kb, h * kb + kb):
            crossing((2 * level + 1 - x) * PARTS + t).wait_recv()

    def half(panel, h):
        return right[pl.ds(panel * PARTS + h * kb, kb)].reshape(kb * side, side)

    def term(pair, j, level, h):
        panel = 2 * level + (x if j == 0 else 1 - x)
        origin = ((w - panel + WIDE) % WIDE) // share
        if h is None:
            tile = jnp.concatenate([half(panel, i) for i in range(HALVES)], axis=1)
        else:
            tile = half(panel, h)
        return jnp.dot(left[origin, pair, j], tile, preferred_element_type=jnp.float32)

    def add(slot, pair, terms, first=False):
        value = None
        for j, level in terms:
            product = term(pair, j, near[level], None)
            value = product if value is None else value + product
        total[slot] = value if first else total[slot] + value

    give, hold = 1 - y, y

    def deliver(c, h, source, target):
        start = pl.multiple_of(n * width + h * side, side)
        return pltpu.make_async_remote_copy(
            src_ref=result.at[source, c, h],
            dst_ref=out.at[:, pl.ds(start, side)],
            send_sem=r_send.at[source, c, h],
            recv_sem=r_recv.at[n, h],
            device_id=(w, target),
            device_id_type=MESH,
        )

    for t in range(PARTS):
        relay(1, t)
    hand_over(give, 0)
    relay(2, 0)
    relay(2, 1)
    hand_over(give, 1)
    relay(2, 2)
    relay(2, 3)
    mate_arrived(give, 0)
    mate_arrived(give, 1)
    diagonal_arrived(give, 0)
    add(0, give, [(0, 0), (0, 1), (0, 2)], first=True)
    relay(3, 0)
    relay(3, 1)
    diagonal_arrived(give, 1)
    for level in range(2):
        for h in range(HALVES):
            peer_arrived(near[level], h)
    add(0, give, [(1, 0), (1, 1)])
    hand_over(hold, 0)
    relay(3, 2)
    relay(3, 3)
    add(0, give, [(0, 3)])
    for h in range(HALVES):
        peer_arrived(near[2], h)
    add(0, give, [(1, 2)])
    mate_arrived(hold, 0)
    mate_arrived(hold, 1)
    diagonal_arrived(hold, 0)
    add(1, hold, [(0, 0), (0, 1), (0, 2), (0, 3)], first=True)
    for h in range(HALVES):
        peer_arrived(near[3], h)
        value = total[0, :, h * side : (h + 1) * side] + term(give, 1, near[3], h)
        for c in range(2):
            q = 2 * give + c
            kept = value[c * side : (c + 1) * side] * keep[h, home(q)].astype(jnp.float32)
            result[0, c, h] = kept.astype(jnp.bfloat16)
            deliver(c, h, 0, q).start()
    hand_over(hold, 1)
    diagonal_arrived(hold, 1)
    add(1, hold, [(1, 0), (1, 1), (1, 2), (1, 3)])
    for h in range(HALVES):
        c = 1 - core
        kept = total[1, pl.ds(pl.multiple_of(c * side, side), side), h * side : (h + 1) * side]
        result[1, 0, h] = (kept * keep[h, home(mate)].astype(jnp.float32)).astype(jnp.bfloat16)
        deliver(0, h, 1, mate).start()
    for h in range(HALVES):
        kept = total[1, pl.ds(pl.multiple_of(core * side, side), side), h * side : (h + 1) * side]
        start = pl.multiple_of(n * width + h * side, side)
        out[:, pl.ds(start, side)] = (kept * keep[h, home(n)].astype(jnp.float32)).astype(
            jnp.bfloat16
        )

    for unit in units:
        to_far(*unit).wait_send()
        to_mate(*unit).wait_send()
        pass_on(*unit).wait_send()
    for t in range(PARTS):
        for step in range(DEPTH):
            from_below = (w - 2 * step) * PARTS + t
            from_above = (w + 2 * step) * PARTS + t

            @pl.when(z - step >= 0)
            def _():
                @pl.when(z < DEPTH - 1)
                def _():
                    upward(from_below).wait_send()

                crossing(from_below).wait_send()

            @pl.when((z + step < DEPTH) & (z > 0))
            def _():
                downward(from_above).wait_send()

            if step > 0:

                @pl.when(z + step < DEPTH)
                def _():
                    crossing(from_above).wait_send()

    for h in range(HALVES):
        for c in range(2):
            deliver(c, h, 0, 2 * give + c).wait_send()
        deliver(0, h, 1, mate).wait_send()
    for origin in (mate, far, diagonal):
        for h in range(HALVES):
            start = pl.multiple_of(origin * width + h * side, side)
            pltpu.make_async_remote_copy(
                src_ref=result.at[0, 0, h],
                dst_ref=out.at[:, pl.ds(start, side)],
                send_sem=r_send.at[0, 0, h],
                recv_sem=r_recv.at[origin, h],
                device_id=(w, origin),
                device_id_type=MESH,
            ).wait_recv()


def fused(a_blocks, a_cols, a_scales, a_counts, b_panel, b_scales, keep_mask, row_perm):
    rows, share, slots, side = a_blocks.shape[:4]
    depth, width = b_panel.shape
    pieces = WIDE * PARTS
    in_place = pl.BlockSpec(memory_space=pltpu.HBM)
    dma = pltpu.SemaphoreType.DMA
    return pl.pallas_call(
        kernel,
        out_shape=pltpu.VMEM((side, width * NARROW), jnp.bfloat16),
        in_specs=[in_place] * 8,
        out_specs=pl.BlockSpec(memory_space=pltpu.VMEM),
        scratch_shapes=[
            pltpu.SMEM((rows, slots, a_cols.shape[1]), jnp.int32),
            pltpu.SMEM((rows, slots, a_cols.shape[1]), jnp.float32),
            pltpu.SMEM(a_counts.shape, jnp.int32),
            pltpu.SMEM(b_scales.shape, jnp.float32),
            pltpu.SMEM((keep_mask.shape[1], rows), jnp.int32),
            pltpu.SMEM(row_perm.shape, jnp.int32),
            dma((6,)),
            pltpu.VMEM(a_blocks.shape, jnp.bfloat16),
            pltpu.VMEM((NARROW, 2, share, 2 * side, depth), jnp.bfloat16),
            pltpu.VMEM((pieces, side, side), jnp.bfloat16),
            pltpu.VMEM((2, 2, HALVES, side, side), jnp.bfloat16),
            pltpu.VMEM((2, 2 * side, width), jnp.float32),
            dma((1 + PARTS,)),
            dma((pieces,)),
            dma((pieces,)),
            dma((pieces,)),
            dma((pieces,)),
            dma((NARROW, 2, share)),
            dma((2, 2, share)),
            dma((2, share)),
            dma((2, 2, HALVES)),
            dma((NARROW, HALVES)),
        ],
        compiler_params=pltpu.CompilerParams(
            collective_id=0, has_side_effects=True, vmem_limit_bytes=60 * 2**20
        ),
    )(
        a_blocks,
        jnp.transpose(a_cols, (0, 2, 1)),
        jnp.transpose(a_scales, (0, 2, 1)),
        a_counts,
        b_panel,
        b_scales,
        jnp.transpose(keep_mask),
        row_perm,
    )


def shifted(block, axis, distance):
    devices = range(lax.axis_size(axis))
    route = [((i - distance) % len(devices), i) for i in devices]
    return lax.ppermute(block, axis, route)


def chosen(table, index):
    tail = (1,) * (table.ndim - 1)
    index = index.reshape(index.shape + tail)
    found = jnp.broadcast_to(table[0], index.shape[: index.ndim - len(tail)] + table.shape[1:])
    for k in range(1, table.shape[0]):
        found = jnp.where(index == k, table[k], found)
    return found


def section_term(row_blocks, slot_cols, weights, b_tiles):
    row_count = row_blocks.shape[0]
    slot_count = row_blocks.shape[1]
    block_side = row_blocks.shape[2]
    scaled = (row_blocks.astype(jnp.float32) * weights[:, :, None, None]).astype(jnp.bfloat16)
    left = jnp.transpose(scaled, (0, 2, 1, 3)).reshape(
        row_count, block_side, slot_count * block_side
    )
    right = chosen(b_tiles, slot_cols.reshape(-1)).reshape(
        row_count, slot_count * block_side, b_tiles.shape[2]
    )
    return jnp.einsum("rik,rkj->rij", left, right, preferred_element_type=jnp.float32)


def by_rings(a_blocks, a_cols, a_scales, a_counts, b_panel, b_scales, keep_mask, row_perm):
    wide_count = lax.axis_size("wide")
    narrow_count = lax.axis_size("narrow")
    device_row = lax.axis_index("wide")
    device_column = lax.axis_index("narrow")
    row_count, section_share, slot_count, block_side = a_blocks.shape[:4]
    section_total = section_share * narrow_count
    k_rows = b_panel.shape[0] // block_side
    out_width = b_panel.shape[1]
    col_blocks = out_width // block_side
    held = [a_blocks]
    for _ in range(narrow_count - 1):
        held.append(shifted(held[-1], "narrow", 1))
    held = jnp.stack(held)
    slot_ids = jnp.arange(slot_count, dtype=jnp.int32)
    accumulated = jnp.zeros((row_count, block_side, out_width), jnp.float32)
    current = b_panel.reshape(k_rows, block_side, out_width)
    for step_number in range(section_total):
        if step_number > 0:
            current = shifted(current, "wide", 1)
        back = (device_column - step_number // section_share) % narrow_count
        row_blocks = lax.dynamic_index_in_dim(held, back, keepdims=False)
        row_blocks = row_blocks[:, step_number % section_share]
        panel_number = (device_row - step_number) % wide_count
        slot_cols = a_cols[:, step_number]
        live_slots = (slot_ids[None, :] < a_counts[:, step_number][:, None]).astype(jnp.float32)
        weights = (
            a_scales[:, step_number]
            * chosen(lax.dynamic_slice(b_scales, (panel_number * k_rows,), (k_rows,)), slot_cols)
            * live_slots
        )
        accumulated = accumulated + section_term(row_blocks, slot_cols, weights, current)
    masked = (
        accumulated.reshape(row_count, block_side, col_blocks, block_side)
        * keep_mask.astype(jnp.float32)[:, None, :, None]
    )
    filtered = masked.astype(jnp.bfloat16).reshape(row_count, block_side, out_width)
    new_order = row_perm[0]
    positions = jnp.arange(row_count, dtype=jnp.int32)
    matches = (new_order[None, :] == positions[:, None]).astype(jnp.int32)
    inverse = jnp.sum(positions[None, :] * matches, axis=1)
    reordered = chosen(filtered, inverse).reshape(row_count * block_side, out_width)
    return lax.all_to_all(reordered, "narrow", split_axis=0, concat_axis=1, tiled=True)


def per_device(*operands):
    wide_count = lax.axis_size("wide")
    narrow_count = lax.axis_size("narrow")
    rows, share, slots, side = operands[0].shape[:4]
    depth, width = operands[4].shape
    fits = rows == 4 and share == 2 and depth == width == 2 * side
    if fits and narrow_count == NARROW and wide_count == WIDE:
        return fused(*operands)
    return by_rings(*operands)


def solution(mesh):
    in_specs = (
        P("wide", "narrow", None, None, None),
        P("wide", None, None),
        P("wide", None, None),
        P("wide", None),
        P("wide", "narrow"),
        P(),
        P("wide", "narrow"),
        P("wide", None),
    )
    out_specs = P(("wide", "narrow"), None)
    return jax.shard_map(
        per_device, mesh=mesh, in_specs=in_specs, out_specs=out_specs, check_vma=False
    )
```

```python
import functools

import jax
import jax.numpy as jnp
from jax import lax
from jax.experimental import pallas as pl
from jax.experimental.pallas import tpu as pltpu
from jax.sharding import PartitionSpec as P

MESH = pl.DeviceIdType.MESH
HALVES = 2
PARTS = 4
LAG = 1
WIDE = 8
DEPTH = 4
NARROW = 4
EARLY = 1


def kernel(
    a_hbm,
    cols_hbm,
    scales_hbm,
    counts_hbm,
    b_hbm,
    b_scales_hbm,
    keep_hbm,
    perm_hbm,
    out,
    cols,
    scales,
    counts,
    b_scales,
    keep,
    perm,
    table_sem,
    a_own,
    left,
    right,
    carry,
    result,
    total,
    load_sem,
    b_recv,
    b_up,
    b_down,
    b_cross,
    k_recv,
    k_down,
    k_mate,
    a_recv,
    a_mate,
    a_far,
    r_send,
    r_recv,
):
    w = lax.axis_index("wide")
    n = lax.axis_index("narrow")
    x = w % 2
    z = w // 2
    y = n // 2
    core = n % 2
    rows, share, slots, side = a_own.shape[:4]
    kb = b_hbm.shape[0] // side
    width = b_hbm.shape[1]
    across = w + 1 - 2 * x
    mate = n + 1 - 2 * core
    far = (n + 2) % 4
    diagonal = 3 - n

    barrier = pltpu.get_barrier_semaphore()
    for peer in ((w, mate), (w, far), (w, diagonal), (across, n)):
        pl.semaphore_signal(barrier, inc=1, device_id=peer, device_id_type=MESH)

    @pl.when(z > 0)
    def _():
        pl.semaphore_signal(barrier, inc=1, device_id=(w - 2, n), device_id_type=MESH)

    @pl.when(z < DEPTH - 1)
    def _():
        pl.semaphore_signal(barrier, inc=1, device_id=(w + 2, n), device_id_type=MESH)

    @pl.when((z == DEPTH - 2) & (core == 1))
    def _():
        pl.semaphore_signal(barrier, inc=1, device_id=(w + 2, mate), device_id_type=MESH)

    @pl.when((z == 0) & (core == 0))
    def _():
        pl.semaphore_signal(barrier, inc=1, device_id=(across, mate), device_id_type=MESH)

    tables = [
        pltpu.make_async_copy(source, kept, table_sem.at[i])
        for i, (source, kept) in enumerate(
            (
                (perm_hbm, perm),
                (cols_hbm, cols),
                (scales_hbm, scales),
                (counts_hbm, counts),
                (b_scales_hbm, b_scales),
                (keep_hbm, keep),
            )
        )
    ]
    for copy in tables:
        copy.start()
    load_a = pltpu.make_async_copy(a_hbm, a_own, load_sem.at[0])
    load_a.start()
    load_b = [
        pltpu.make_async_copy(
            b_hbm.at[t % kb * side : (t % kb + 1) * side, t // kb * side : (t // kb + 1) * side],
            right.at[w * PARTS + t],
            load_sem.at[1 + t],
        )
        for t in range(PARTS)
    ]
    for copy in load_b:
        copy.start()

    def piece(slot, sent, target):
        return pltpu.make_async_remote_copy(
            src_ref=right.at[slot],
            dst_ref=right.at[slot],
            send_sem=sent.at[slot],
            recv_sem=b_recv.at[slot],
            device_id=(target, n),
            device_id_type=MESH,
        )

    def upward(slot):
        return piece(slot, b_up, w + 2)

    def downward(slot):
        return piece(slot, b_down, w - 2)

    def crossing(slot):
        return piece(slot, b_cross, across)

    def top_slot(t):
        return (2 * (DEPTH - 1) + x) * PARTS + t

    def lift(t, source, target, sent, landed, wide, narrow):
        return pltpu.make_async_remote_copy(
            src_ref=source,
            dst_ref=target,
            send_sem=sent,
            recv_sem=landed,
            device_id=(wide, narrow),
            device_id_type=MESH,
        )

    def enter(t):
        slot = w * PARTS + t
        return lift(t, right.at[slot], carry.at[t], b_down.at[slot], k_recv.at[t], w - 2, mate)

    def carry_down(t):
        return lift(t, carry.at[t], carry.at[t], k_down.at[t], k_recv.at[t], w - 2, n)

    def carry_mate(t):
        slot = top_slot(t)
        return lift(t, carry.at[t], right.at[slot], k_mate.at[t], b_recv.at[slot], w, mate)

    def carry_cross(t):
        slot = top_slot(t)
        return lift(t, carry.at[t], right.at[slot], k_down.at[t], b_recv.at[slot], across, mate)

    def block(origin, pair, j, sent, target):
        return pltpu.make_async_remote_copy(
            src_ref=left.at[origin, pair, j],
            dst_ref=left.at[origin, pair, j],
            send_sem=sent,
            recv_sem=a_recv.at[origin, pair, j],
            device_id=(w, target),
            device_id_type=MESH,
        )

    def to_far(pair, j):
        return block(n, pair, j, a_far.at[pair, j], far)

    def to_mate(pair, j):
        return block(n, pair, j, a_mate.at[0, pair, j], mate)

    def from_far(pair, j):
        return block(far, pair, j, a_far.at[pair, j], far)

    def pass_on(pair, j):
        return block(far, pair, j, a_mate.at[1, pair, j], mate)

    def home(q):
        found = jnp.int32(0)
        for r in range(rows):
            found = jnp.where(perm[0, r] == q, r, found)
        return found

    def scale(pair, j):
        s = n * share + j
        panel = (w - s + WIDE) % WIDE
        for c in range(2):
            r = home(2 * pair + c)
            weights, places = [], []
            for m in range(slots):
                place = cols[r, m, s]
                live = jnp.where(m < counts[r, s], 1.0, 0.0)
                weights.append(scales[r, m, s] * b_scales[panel * kb + place] * live)
                places.append(place)
            for k in range(kb):
                value = None
                for m in range(slots):
                    weight = jnp.where(places[m] == k, weights[m], 0.0)
                    term = a_own[r, j, m].astype(jnp.float32) * weight
                    value = term if value is None else value + term
                left[n, pair, j, c * side : (c + 1) * side, k * side : (k + 1) * side] = (
                    value.astype(jnp.bfloat16)
                )

    pairs = (y, 1 - y)
    units = [(pair, j) for pair in pairs for j in range(share)]
    for copy in tables:
        copy.wait()
    load_a.wait()
    for unit in units[:EARLY]:
        scale(*unit)
    for copy in load_b:
        copy.wait()

    neighbours = jnp.where(z > 0, 1, 0) + jnp.where(z < DEPTH - 1, 1, 0)
    lifted = ((z == DEPTH - 1) & (core == 0)) | ((z == 0) & (core == 1))
    pl.semaphore_wait(barrier, 4 + neighbours + jnp.where(lifted, 1, 0))

    for unit in units[:EARLY]:
        to_far(*unit).start()
    for t in range(PARTS):
        own = w * PARTS + t
        crossing(own).start()

        @pl.when(z < DEPTH - 1)
        def _():
            upward(own).start()

        @pl.when((z > 0) & ((z < DEPTH - 1) | (core == 1)))
        def _():
            downward(own).start()

        @pl.when((z == DEPTH - 1) & (core == 0))
        def _():
            enter(t).start()

    for unit in units[:EARLY]:
        to_mate(*unit).start()
    for unit in units[EARLY:]:
        scale(*unit)
        to_far(*unit).start()
        to_mate(*unit).start()

    def relay(step, t):
        from_below = (w - 2 * step) * PARTS + t
        from_above = (w + 2 * step) * PARTS + t

        @pl.when(z - step >= 0)
        def _():
            upward(from_below).wait_recv()

            @pl.when(z < DEPTH - 1)
            def _():
                upward(from_below).start()

            crossing(from_below).start()

        @pl.when(z + step < DEPTH)
        def _():
            downward(from_above).wait_recv()

            @pl.when((z > 0) & ((z + step < DEPTH - 1) | (core == 1)))
            def _():
                downward(from_above).start()

            @pl.when((z > 0) | (step < DEPTH - 1) | (core == 1))
            def _():
                crossing(from_above).start()

    def ferry(step, t):
        @pl.when((z + step == DEPTH - 1) & (core == 1))
        def _():
            carry_down(t).wait_recv()
            if step < DEPTH - 1:
                carry_down(t).start()
            else:
                carry_cross(t).start()
            carry_mate(t).start()

    def hand_over(pair, j):
        from_far(pair, j).wait_recv()
        pass_on(pair, j).start()

    def mate_arrived(pair, j):
        block(mate, pair, j, a_mate.at[0, pair, j], mate).wait_recv()

    def diagonal_arrived(pair, j):
        block(diagonal, pair, j, a_mate.at[1, pair, j], mate).wait_recv()

    near = (
        z,
        jnp.where(z == 0, 1, z - 1),
        jnp.where(z == 0, 2, jnp.where(z == 3, 1, z + 1)),
        jnp.where(z < 2, 3, 0),
    )

    def peer_arrived(level, h):
        for t in range(h * kb, h * kb + kb):
            crossing((2 * level + 1 - x) * PARTS + t).wait_recv()

    def half(panel, h):
        return right[pl.ds(panel * PARTS + h * kb, kb)].reshape(kb * side, side)

    def term(pair, j, level, h):
        panel = 2 * level + (x if j == 0 else 1 - x)
        origin = ((w - panel + WIDE) % WIDE) // share
        if h is None:
            tile = jnp.concatenate([half(panel, i) for i in range(HALVES)], axis=1)
        else:
            tile = half(panel, h)
        return jnp.dot(left[origin, pair, j], tile, preferred_element_type=jnp.float32)

    def add(slot, pair, terms, first=False):
        value = None
        for j, level in terms:
            product = term(pair, j, near[level], None)
            value = product if value is None else value + product
        total[slot] = value if first else total[slot] + value

    give, hold = 1 - y, y

    def deliver(c, h, source, target):
        start = pl.multiple_of(n * width + h * side, side)
        return pltpu.make_async_remote_copy(
            src_ref=result.at[source, c, h],
            dst_ref=out.at[:, pl.ds(start, side)],
            send_sem=r_send.at[source, c, h],
            recv_sem=r_recv.at[n, h],
            device_id=(w, target),
            device_id_type=MESH,
        )

    for t in range(PARTS):
        relay(1, t)
        if t >= LAG:
            ferry(1, t - LAG)
    for t in range(PARTS - LAG, PARTS):
        ferry(1, t)
    hand_over(give, 0)
    for t in range(PARTS):
        ferry(2, t)
        relay(2, t)
        if t == 1:
            hand_over(give, 1)
    mate_arrived(give, 0)
    mate_arrived(give, 1)
    diagonal_arrived(give, 0)
    add(0, give, [(0, 0), (0, 1), (0, 2)], first=True)
    for t in range(PARTS // 2):
        ferry(3, t)
        relay(3, t)
    diagonal_arrived(give, 1)
    for level in range(2):
        for h in range(HALVES):
            peer_arrived(near[level], h)
    add(0, give, [(1, 0), (1, 1)])
    hand_over(hold, 0)
    for t in range(PARTS // 2, PARTS):
        ferry(3, t)
        relay(3, t)
    add(0, give, [(0, 3)])
    for h in range(HALVES):
        peer_arrived(near[2], h)
    add(0, give, [(1, 2)])
    mate_arrived(hold, 0)
    mate_arrived(hold, 1)
    diagonal_arrived(hold, 0)
    add(1, hold, [(0, 0), (0, 1), (0, 2), (0, 3)], first=True)
    for h in range(HALVES):
        if h == 1:
            hand_over(hold, 1)
        peer_arrived(near[3], h)
        value = total[0, :, h * side : (h + 1) * side] + term(give, 1, near[3], h)
        for c in range(2):
            q = 2 * give + c
            kept = value[c * side : (c + 1) * side] * keep[h, home(q)].astype(jnp.float32)
            result[0, c, h] = kept.astype(jnp.bfloat16)
            deliver(c, h, 0, q).start()
    diagonal_arrived(hold, 1)
    add(1, hold, [(1, 0), (1, 1), (1, 2), (1, 3)])
    for h in range(HALVES):
        c = 1 - core
        kept = total[1, pl.ds(pl.multiple_of(c * side, side), side), h * side : (h + 1) * side]
        result[1, 0, h] = (kept * keep[h, home(mate)].astype(jnp.float32)).astype(jnp.bfloat16)
        deliver(0, h, 1, mate).start()
    for h in range(HALVES):
        kept = total[1, pl.ds(pl.multiple_of(core * side, side), side), h * side : (h + 1) * side]
        start = pl.multiple_of(n * width + h * side, side)
        out[:, pl.ds(start, side)] = (kept * keep[h, home(n)].astype(jnp.float32)).astype(
            jnp.bfloat16
        )

    for unit in units:
        to_far(*unit).wait_send()
        to_mate(*unit).wait_send()
        pass_on(*unit).wait_send()
    for t in range(PARTS):
        for step in range(DEPTH):
            from_below = (w - 2 * step) * PARTS + t
            from_above = (w + 2 * step) * PARTS + t

            @pl.when(z - step >= 0)
            def _():
                @pl.when(z < DEPTH - 1)
                def _():
                    upward(from_below).wait_send()

                crossing(from_below).wait_send()

            passed = (z + step < DEPTH - 1) | (core == 1) | (step == 0)

            @pl.when((z + step < DEPTH) & (z > 0) & passed)
            def _():
                downward(from_above).wait_send()

            if step > 0:

                @pl.when((z + step < DEPTH) & ((z > 0) | (step < DEPTH - 1) | (core == 1)))
                def _():
                    crossing(from_above).wait_send()

    @pl.when((z < DEPTH - 1) & (core == 1))
    def _():
        for t in range(PARTS):
            carry_down(t).wait_send()
            carry_mate(t).wait_send()

    for h in range(HALVES):
        for c in range(2):
            deliver(c, h, 0, 2 * give + c).wait_send()
        deliver(0, h, 1, mate).wait_send()
    for origin in (mate, far, diagonal):
        for h in range(HALVES):
            start = pl.multiple_of(origin * width + h * side, side)
            pltpu.make_async_remote_copy(
                src_ref=result.at[0, 0, h],
                dst_ref=out.at[:, pl.ds(start, side)],
                send_sem=r_send.at[0, 0, h],
                recv_sem=r_recv.at[origin, h],
                device_id=(w, origin),
                device_id_type=MESH,
            ).wait_recv()


def fused(a_blocks, a_cols, a_scales, a_counts, b_panel, b_scales, keep_mask, row_perm):
    rows, share, slots, side = a_blocks.shape[:4]
    depth, width = b_panel.shape
    pieces = WIDE * PARTS
    in_place = pl.BlockSpec(memory_space=pltpu.HBM)
    dma = pltpu.SemaphoreType.DMA
    return pl.pallas_call(
        kernel,
        out_shape=pltpu.VMEM((side, width * NARROW), jnp.bfloat16),
        in_specs=[in_place] * 8,
        out_specs=pl.BlockSpec(memory_space=pltpu.VMEM),
        scratch_shapes=[
            pltpu.SMEM((rows, slots, a_cols.shape[1]), jnp.int32),
            pltpu.SMEM((rows, slots, a_cols.shape[1]), jnp.float32),
            pltpu.SMEM(a_counts.shape, jnp.int32),
            pltpu.SMEM(b_scales.shape, jnp.float32),
            pltpu.SMEM((keep_mask.shape[1], rows), jnp.int32),
            pltpu.SMEM(row_perm.shape, jnp.int32),
            dma((6,)),
            pltpu.VMEM(a_blocks.shape, jnp.bfloat16),
            pltpu.VMEM((NARROW, 2, share, 2 * side, depth), jnp.bfloat16),
            pltpu.VMEM((pieces, side, side), jnp.bfloat16),
            pltpu.VMEM((PARTS, side, side), jnp.bfloat16),
            pltpu.VMEM((2, 2, HALVES, side, side), jnp.bfloat16),
            pltpu.VMEM((2, 2 * side, width), jnp.float32),
            dma((1 + PARTS,)),
            dma((pieces,)),
            dma((pieces,)),
            dma((pieces,)),
            dma((pieces,)),
            dma((PARTS,)),
            dma((PARTS,)),
            dma((PARTS,)),
            dma((NARROW, 2, share)),
            dma((2, 2, share)),
            dma((2, share)),
            dma((2, 2, HALVES)),
            dma((NARROW, HALVES)),
        ],
        compiler_params=pltpu.CompilerParams(
            collective_id=0, has_side_effects=True, vmem_limit_bytes=60 * 2**20
        ),
    )(
        a_blocks,
        jnp.transpose(a_cols, (0, 2, 1)),
        jnp.transpose(a_scales, (0, 2, 1)),
        a_counts,
        b_panel,
        b_scales,
        jnp.transpose(keep_mask),
        row_perm,
    )


def shifted(block, axis, distance):
    devices = range(lax.axis_size(axis))
    route = [((i - distance) % len(devices), i) for i in devices]
    return lax.ppermute(block, axis, route)


def chosen(table, index):
    tail = (1,) * (table.ndim - 1)
    index = index.reshape(index.shape + tail)
    found = jnp.broadcast_to(table[0], index.shape[: index.ndim - len(tail)] + table.shape[1:])
    for k in range(1, table.shape[0]):
        found = jnp.where(index == k, table[k], found)
    return found


def section_term(row_blocks, slot_cols, weights, b_tiles):
    row_count = row_blocks.shape[0]
    slot_count = row_blocks.shape[1]
    block_side = row_blocks.shape[2]
    scaled = (row_blocks.astype(jnp.float32) * weights[:, :, None, None]).astype(jnp.bfloat16)
    left = jnp.transpose(scaled, (0, 2, 1, 3)).reshape(
        row_count, block_side, slot_count * block_side
    )
    right = chosen(b_tiles, slot_cols.reshape(-1)).reshape(
        row_count, slot_count * block_side, b_tiles.shape[2]
    )
    return jnp.einsum("rik,rkj->rij", left, right, preferred_element_type=jnp.float32)


def by_rings(a_blocks, a_cols, a_scales, a_counts, b_panel, b_scales, keep_mask, row_perm):
    wide_count = lax.axis_size("wide")
    narrow_count = lax.axis_size("narrow")
    device_row = lax.axis_index("wide")
    device_column = lax.axis_index("narrow")
    row_count, section_share, slot_count, block_side = a_blocks.shape[:4]
    section_total = section_share * narrow_count
    k_rows = b_panel.shape[0] // block_side
    out_width = b_panel.shape[1]
    col_blocks = out_width // block_side
    held = [a_blocks]
    for _ in range(narrow_count - 1):
        held.append(shifted(held[-1], "narrow", 1))
    held = jnp.stack(held)
    slot_ids = jnp.arange(slot_count, dtype=jnp.int32)
    accumulated = jnp.zeros((row_count, block_side, out_width), jnp.float32)
    current = b_panel.reshape(k_rows, block_side, out_width)
    for step_number in range(section_total):
        if step_number > 0:
            current = shifted(current, "wide", 1)
        back = (device_column - step_number // section_share) % narrow_count
        row_blocks = lax.dynamic_index_in_dim(held, back, keepdims=False)
        row_blocks = row_blocks[:, step_number % section_share]
        panel_number = (device_row - step_number) % wide_count
        slot_cols = a_cols[:, step_number]
        live_slots = (slot_ids[None, :] < a_counts[:, step_number][:, None]).astype(jnp.float32)
        weights = (
            a_scales[:, step_number]
            * chosen(lax.dynamic_slice(b_scales, (panel_number * k_rows,), (k_rows,)), slot_cols)
            * live_slots
        )
        accumulated = accumulated + section_term(row_blocks, slot_cols, weights, current)
    masked = (
        accumulated.reshape(row_count, block_side, col_blocks, block_side)
        * keep_mask.astype(jnp.float32)[:, None, :, None]
    )
    filtered = masked.astype(jnp.bfloat16).reshape(row_count, block_side, out_width)
    new_order = row_perm[0]
    positions = jnp.arange(row_count, dtype=jnp.int32)
    matches = (new_order[None, :] == positions[:, None]).astype(jnp.int32)
    inverse = jnp.sum(positions[None, :] * matches, axis=1)
    reordered = chosen(filtered, inverse).reshape(row_count * block_side, out_width)
    return lax.all_to_all(reordered, "narrow", split_axis=0, concat_axis=1, tiled=True)


def per_device(*operands):
    wide_count = lax.axis_size("wide")
    narrow_count = lax.axis_size("narrow")
    rows, share, slots, side = operands[0].shape[:4]
    depth, width = operands[4].shape
    fits = rows == 4 and share == 2 and depth == width == 2 * side
    if fits and narrow_count == NARROW and wide_count == WIDE:
        return fused(*operands)
    return by_rings(*operands)


def solution(mesh):
    in_specs = (
        P("wide", "narrow", None, None, None),
        P("wide", None, None),
        P("wide", None, None),
        P("wide", None),
        P("wide", "narrow"),
        P(),
        P("wide", "narrow"),
        P("wide", None),
    )
    out_specs = P(("wide", "narrow"), None)
    return jax.shard_map(
        per_device, mesh=mesh, in_specs=in_specs, out_specs=out_specs, check_vma=False
    )
```

```python
import functools

import jax
import jax.numpy as jnp
from jax import lax
from jax.experimental import pallas as pl
from jax.experimental.pallas import tpu as pltpu
from jax.sharding import PartitionSpec as P

MESH = pl.DeviceIdType.MESH
HALVES = 2
PARTS = 4
LAG = 1
WIDE = 8
DEPTH = 4
NARROW = 4
EARLY = 1


def kernel(
    a_hbm,
    cols_hbm,
    scales_hbm,
    counts_hbm,
    b_hbm,
    b_scales_hbm,
    keep_hbm,
    perm_hbm,
    out,
    cols,
    scales,
    counts,
    b_scales,
    keep,
    perm,
    table_sem,
    a_own,
    left,
    right,
    carry,
    result,
    total,
    load_sem,
    b_recv,
    b_up,
    b_down,
    b_cross,
    k_recv,
    k_down,
    k_mate,
    a_recv,
    a_mate,
    a_far,
    r_send,
    r_recv,
):
    w = lax.axis_index("wide")
    n = lax.axis_index("narrow")
    x = w % 2
    z = w // 2
    y = n // 2
    core = n % 2
    rows, share, slots, side = a_own.shape[:4]
    kb = b_hbm.shape[0] // side
    width = b_hbm.shape[1]
    across = w + 1 - 2 * x
    mate = n + 1 - 2 * core
    far = (n + 2) % 4
    diagonal = 3 - n

    barrier = pltpu.get_barrier_semaphore()
    for peer in ((w, mate), (w, far), (w, diagonal), (across, n)):
        pl.semaphore_signal(barrier, inc=1, device_id=peer, device_id_type=MESH)

    @pl.when(z > 0)
    def _():
        pl.semaphore_signal(barrier, inc=1, device_id=(w - 2, n), device_id_type=MESH)

    @pl.when(z < DEPTH - 1)
    def _():
        pl.semaphore_signal(barrier, inc=1, device_id=(w + 2, n), device_id_type=MESH)

    @pl.when((z == DEPTH - 2) & (core == 1))
    def _():
        pl.semaphore_signal(barrier, inc=1, device_id=(w + 2, mate), device_id_type=MESH)

    @pl.when((z == 0) & (core == 0))
    def _():
        pl.semaphore_signal(barrier, inc=1, device_id=(across, mate), device_id_type=MESH)

    tables = [
        pltpu.make_async_copy(source, kept, table_sem.at[i])
        for i, (source, kept) in enumerate(
            (
                (perm_hbm, perm),
                (cols_hbm, cols),
                (scales_hbm, scales),
                (counts_hbm, counts),
                (b_scales_hbm, b_scales),
                (keep_hbm, keep),
            )
        )
    ]
    for copy in tables:
        copy.start()
    load_a = pltpu.make_async_copy(a_hbm, a_own, load_sem.at[0])
    load_a.start()
    load_b = [
        pltpu.make_async_copy(
            b_hbm.at[t % kb * side : (t % kb + 1) * side, t // kb * side : (t // kb + 1) * side],
            right.at[w * PARTS + t],
            load_sem.at[1 + t],
        )
        for t in range(PARTS)
    ]
    for copy in load_b:
        copy.start()

    def piece(slot, sent, target):
        return pltpu.make_async_remote_copy(
            src_ref=right.at[slot],
            dst_ref=right.at[slot],
            send_sem=sent.at[0],
            recv_sem=b_recv.at[slot],
            device_id=(target, n),
            device_id_type=MESH,
        )

    def upward(slot):
        return piece(slot, b_up, w + 2)

    def downward(slot):
        return piece(slot, b_down, w - 2)

    def crossing(slot):
        return piece(slot, b_cross, across)

    def top_slot(t):
        return (2 * (DEPTH - 1) + x) * PARTS + t

    def lift(t, source, target, sent, landed, wide, narrow):
        return pltpu.make_async_remote_copy(
            src_ref=source,
            dst_ref=target,
            send_sem=sent,
            recv_sem=landed,
            device_id=(wide, narrow),
            device_id_type=MESH,
        )

    def enter(t):
        slot = w * PARTS + t
        return lift(t, right.at[slot], carry.at[t], b_down.at[0], k_recv.at[t], w - 2, mate)

    def carry_down(t):
        return lift(t, carry.at[t], carry.at[t], k_down.at[0], k_recv.at[t], w - 2, n)

    def carry_mate(t):
        slot = top_slot(t)
        return lift(t, carry.at[t], right.at[slot], k_mate.at[0], b_recv.at[slot], w, mate)

    def carry_cross(t):
        slot = top_slot(t)
        return lift(t, carry.at[t], right.at[slot], k_down.at[0], b_recv.at[slot], across, mate)

    def block(origin, pair, j, sent, target):
        return pltpu.make_async_remote_copy(
            src_ref=left.at[origin, pair, j],
            dst_ref=left.at[origin, pair, j],
            send_sem=sent,
            recv_sem=a_recv.at[origin, pair, j],
            device_id=(w, target),
            device_id_type=MESH,
        )

    def to_far(pair, j):
        return block(n, pair, j, a_far.at[0], far)

    def to_mate(pair, j):
        return block(n, pair, j, a_mate.at[0], mate)

    def from_far(pair, j):
        return block(far, pair, j, a_far.at[0], far)

    def pass_on(pair, j):
        return block(far, pair, j, a_mate.at[1], mate)

    def home(q):
        found = jnp.int32(0)
        for r in range(rows):
            found = jnp.where(perm[0, r] == q, r, found)
        return found

    def scale(pair, j):
        s = n * share + j
        panel = (w - s + WIDE) % WIDE
        for c in range(2):
            r = home(2 * pair + c)
            weights, places = [], []
            for m in range(slots):
                place = cols[r, m, s]
                live = jnp.where(m < counts[r, s], 1.0, 0.0)
                weights.append(scales[r, m, s] * b_scales[panel * kb + place] * live)
                places.append(place)
            for k in range(kb):
                value = None
                for m in range(slots):
                    weight = jnp.where(places[m] == k, weights[m], 0.0)
                    term = a_own[r, j, m].astype(jnp.float32) * weight
                    value = term if value is None else value + term
                left[n, pair, j, c * side : (c + 1) * side, k * side : (k + 1) * side] = (
                    value.astype(jnp.bfloat16)
                )

    pairs = (y, 1 - y)
    units = [(pair, j) for pair in pairs for j in range(share)]
    for copy in tables:
        copy.wait()
    load_a.wait()
    for unit in units[:EARLY]:
        scale(*unit)
    for copy in load_b:
        copy.wait()

    neighbours = jnp.where(z > 0, 1, 0) + jnp.where(z < DEPTH - 1, 1, 0)
    lifted = ((z == DEPTH - 1) & (core == 0)) | ((z == 0) & (core == 1))
    pl.semaphore_wait(barrier, 4 + neighbours + jnp.where(lifted, 1, 0))

    @pl.when((z == DEPTH - 1) & (core == 0))
    def _():
        for t in range(PARTS):
            enter(t).start()

    @pl.when((z == DEPTH - 1) & (core == 1))
    def _():
        for t in range(PARTS):
            downward(w * PARTS + t).start()

    for unit in units[:EARLY]:
        to_far(*unit).start()
    for t in range(PARTS):
        own = w * PARTS + t

        @pl.when(z < DEPTH - 1)
        def _():
            upward(own).start()

        @pl.when((z > 0) & (z < DEPTH - 1))
        def _():
            downward(own).start()

        crossing(own).start()

    for unit in units[:EARLY]:
        to_mate(*unit).start()
    for unit in units[EARLY:]:
        scale(*unit)
        to_far(*unit).start()
        to_mate(*unit).start()

    def relay(step, t):
        from_below = (w - 2 * step) * PARTS + t
        from_above = (w + 2 * step) * PARTS + t

        @pl.when(z - step >= 0)
        def _():
            upward(from_below).wait_recv()

            @pl.when(z < DEPTH - 1)
            def _():
                upward(from_below).start()

            crossing(from_below).start()

        @pl.when(z + step < DEPTH)
        def _():
            downward(from_above).wait_recv()

            @pl.when((z > 0) & ((z + step < DEPTH - 1) | (core == 1)))
            def _():
                downward(from_above).start()

            @pl.when((z > 0) | (step < DEPTH - 1) | (core == 1))
            def _():
                crossing(from_above).start()

    def ferry(step, t):
        @pl.when((z + step == DEPTH - 1) & (core == 1))
        def _():
            carry_down(t).wait_recv()
            if step < DEPTH - 1:
                carry_down(t).start()
            else:
                carry_cross(t).start()
            carry_mate(t).start()

    def hand_over(pair, j):
        from_far(pair, j).wait_recv()
        pass_on(pair, j).start()

    def mate_arrived(pair, j):
        block(mate, pair, j, a_mate.at[0], mate).wait_recv()

    def diagonal_arrived(pair, j):
        block(diagonal, pair, j, a_mate.at[1], mate).wait_recv()

    near = (
        z,
        jnp.where(z == 0, 1, z - 1),
        jnp.where(z == 0, 2, jnp.where(z == 3, 1, z + 1)),
        jnp.where(z < 2, 3, 0),
    )

    def peer_arrived(level, h):
        for t in range(h * kb, h * kb + kb):
            crossing((2 * level + 1 - x) * PARTS + t).wait_recv()

    def half(panel, h):
        return right[pl.ds(panel * PARTS + h * kb, kb)].reshape(kb * side, side)

    def term(pair, j, level, h):
        panel = 2 * level + (x if j == 0 else 1 - x)
        origin = ((w - panel + WIDE) % WIDE) // share
        if h is None:
            tile = jnp.concatenate([half(panel, i) for i in range(HALVES)], axis=1)
        else:
            tile = half(panel, h)
        return jnp.dot(left[origin, pair, j], tile, preferred_element_type=jnp.float32)

    def add(slot, pair, terms, first=False):
        value = None
        for j, level in terms:
            product = term(pair, j, near[level], None)
            value = product if value is None else value + product
        total[slot] = value if first else total[slot] + value

    give, hold = 1 - y, y

    def deliver(c, h, source, target):
        start = pl.multiple_of(n * width + h * side, side)
        return pltpu.make_async_remote_copy(
            src_ref=result.at[source, c, h],
            dst_ref=out.at[:, pl.ds(start, side)],
            send_sem=r_send.at[source],
            recv_sem=r_recv.at[n, h],
            device_id=(w, target),
            device_id_type=MESH,
        )

    for t in range(PARTS):
        relay(1, t)
        if t >= LAG:
            ferry(1, t - LAG)
    for t in range(PARTS - LAG, PARTS):
        ferry(1, t)
    hand_over(give, 0)
    for t in range(PARTS):
        ferry(2, t)
        relay(2, t)
        if t == 1:
            hand_over(give, 1)
    mate_arrived(give, 0)
    mate_arrived(give, 1)
    diagonal_arrived(give, 0)
    add(0, give, [(0, 0), (0, 1), (0, 2)], first=True)
    for t in range(PARTS // 2):
        ferry(3, t)
        relay(3, t)
    diagonal_arrived(give, 1)
    for level in range(2):
        for h in range(HALVES):
            peer_arrived(near[level], h)
    add(0, give, [(1, 0), (1, 1)])
    hand_over(hold, 0)
    for t in range(PARTS // 2, PARTS):
        ferry(3, t)
        relay(3, t)
    add(0, give, [(0, 3)])
    for h in range(HALVES):
        peer_arrived(near[2], h)
    add(0, give, [(1, 2)])
    for h in range(HALVES):
        if h == 1:
            hand_over(hold, 1)
        peer_arrived(near[3], h)
        value = total[0, :, h * side : (h + 1) * side] + term(give, 1, near[3], h)
        for c in range(2):
            q = 2 * give + c
            kept = value[c * side : (c + 1) * side] * keep[h, home(q)].astype(jnp.float32)
            result[0, c, h] = kept.astype(jnp.bfloat16)
            deliver(c, h, 0, q).start()
    mate_arrived(hold, 0)
    mate_arrived(hold, 1)
    diagonal_arrived(hold, 0)
    add(1, hold, [(0, 0), (0, 1), (0, 2), (0, 3)], first=True)
    diagonal_arrived(hold, 1)
    add(1, hold, [(1, 0), (1, 1), (1, 2), (1, 3)])
    for h in range(HALVES):
        c = 1 - core
        kept = total[1, pl.ds(pl.multiple_of(c * side, side), side), h * side : (h + 1) * side]
        result[1, 0, h] = (kept * keep[h, home(mate)].astype(jnp.float32)).astype(jnp.bfloat16)
        deliver(0, h, 1, mate).start()
    for h in range(HALVES):
        kept = total[1, pl.ds(pl.multiple_of(core * side, side), side), h * side : (h + 1) * side]
        start = pl.multiple_of(n * width + h * side, side)
        out[:, pl.ds(start, side)] = (kept * keep[h, home(n)].astype(jnp.float32)).astype(
            jnp.bfloat16
        )

    def drain(source, sem):
        pltpu.make_async_remote_copy(
            src_ref=source,
            dst_ref=source,
            send_sem=sem,
            recv_sem=b_recv.at[0],
            device_id=(w, mate),
            device_id_type=MESH,
        ).wait_send()

    for sem in (a_far.at[0], a_mate.at[0], a_mate.at[1]):
        drain(left.at[n], sem)
    for k in range(DEPTH):
        for c in range(2):

            @pl.when((z == k) & (core == c))
            def _(k=k, c=c):
                if k < DEPTH - 1:
                    drain(right.at[pl.ds(0, PARTS * (k + 1))], b_up.at[0])
                if k > 0:
                    levels = DEPTH - k if c == 1 else max(DEPTH - 1 - k, 1)
                    drain(right.at[pl.ds(0, PARTS * levels)], b_down.at[0])
                levels = DEPTH if c == 1 or k > 0 else DEPTH - 1
                drain(right.at[pl.ds(0, PARTS * levels)], b_cross.at[0])
                if c == 1 and k < DEPTH - 1:
                    drain(right.at[pl.ds(0, PARTS)], k_down.at[0])
                    drain(right.at[pl.ds(0, PARTS)], k_mate.at[0])

    drain(result.at[0], r_send.at[0])
    drain(result.at[1, 0], r_send.at[1])
    for origin in (mate, far, diagonal):
        for h in range(HALVES):
            start = pl.multiple_of(origin * width + h * side, side)
            pltpu.make_async_remote_copy(
                src_ref=result.at[0, 0, h],
                dst_ref=out.at[:, pl.ds(start, side)],
                send_sem=r_send.at[0],
                recv_sem=r_recv.at[origin, h],
                device_id=(w, origin),
                device_id_type=MESH,
            ).wait_recv()


def fused(a_blocks, a_cols, a_scales, a_counts, b_panel, b_scales, keep_mask, row_perm):
    rows, share, slots, side = a_blocks.shape[:4]
    depth, width = b_panel.shape
    pieces = WIDE * PARTS
    in_place = pl.BlockSpec(memory_space=pltpu.HBM)
    dma = pltpu.SemaphoreType.DMA
    return pl.pallas_call(
        kernel,
        out_shape=pltpu.VMEM((side, width * NARROW), jnp.bfloat16),
        in_specs=[in_place] * 8,
        out_specs=pl.BlockSpec(memory_space=pltpu.VMEM),
        scratch_shapes=[
            pltpu.SMEM((rows, slots, a_cols.shape[1]), jnp.int32),
            pltpu.SMEM((rows, slots, a_cols.shape[1]), jnp.float32),
            pltpu.SMEM(a_counts.shape, jnp.int32),
            pltpu.SMEM(b_scales.shape, jnp.float32),
            pltpu.SMEM((keep_mask.shape[1], rows), jnp.int32),
            pltpu.SMEM(row_perm.shape, jnp.int32),
            dma((6,)),
            pltpu.VMEM(a_blocks.shape, jnp.bfloat16),
            pltpu.VMEM((NARROW, 2, share, 2 * side, depth), jnp.bfloat16),
            pltpu.VMEM((pieces, side, side), jnp.bfloat16),
            pltpu.VMEM((PARTS, side, side), jnp.bfloat16),
            pltpu.VMEM((2, 2, HALVES, side, side), jnp.bfloat16),
            pltpu.VMEM((2, 2 * side, width), jnp.float32),
            dma((1 + PARTS,)),
            dma((pieces,)),
            dma((1,)),
            dma((1,)),
            dma((1,)),
            dma((PARTS,)),
            dma((1,)),
            dma((1,)),
            dma((NARROW, 2, share)),
            dma((2,)),
            dma((1,)),
            dma((2,)),
            dma((NARROW, HALVES)),
        ],
        compiler_params=pltpu.CompilerParams(
            collective_id=0, has_side_effects=True, vmem_limit_bytes=60 * 2**20
        ),
    )(
        a_blocks,
        jnp.transpose(a_cols, (0, 2, 1)),
        jnp.transpose(a_scales, (0, 2, 1)),
        a_counts,
        b_panel,
        b_scales,
        jnp.transpose(keep_mask),
        row_perm,
    )


def shifted(block, axis, distance):
    devices = range(lax.axis_size(axis))
    route = [((i - distance) % len(devices), i) for i in devices]
    return lax.ppermute(block, axis, route)


def chosen(table, index):
    tail = (1,) * (table.ndim - 1)
    index = index.reshape(index.shape + tail)
    found = jnp.broadcast_to(table[0], index.shape[: index.ndim - len(tail)] + table.shape[1:])
    for k in range(1, table.shape[0]):
        found = jnp.where(index == k, table[k], found)
    return found


def section_term(row_blocks, slot_cols, weights, b_tiles):
    row_count = row_blocks.shape[0]
    slot_count = row_blocks.shape[1]
    block_side = row_blocks.shape[2]
    scaled = (row_blocks.astype(jnp.float32) * weights[:, :, None, None]).astype(jnp.bfloat16)
    left = jnp.transpose(scaled, (0, 2, 1, 3)).reshape(
        row_count, block_side, slot_count * block_side
    )
    right = chosen(b_tiles, slot_cols.reshape(-1)).reshape(
        row_count, slot_count * block_side, b_tiles.shape[2]
    )
    return jnp.einsum("rik,rkj->rij", left, right, preferred_element_type=jnp.float32)


def by_rings(a_blocks, a_cols, a_scales, a_counts, b_panel, b_scales, keep_mask, row_perm):
    wide_count = lax.axis_size("wide")
    narrow_count = lax.axis_size("narrow")
    device_row = lax.axis_index("wide")
    device_column = lax.axis_index("narrow")
    row_count, section_share, slot_count, block_side = a_blocks.shape[:4]
    section_total = section_share * narrow_count
    k_rows = b_panel.shape[0] // block_side
    out_width = b_panel.shape[1]
    col_blocks = out_width // block_side
    held = [a_blocks]
    for _ in range(narrow_count - 1):
        held.append(shifted(held[-1], "narrow", 1))
    held = jnp.stack(held)
    slot_ids = jnp.arange(slot_count, dtype=jnp.int32)
    accumulated = jnp.zeros((row_count, block_side, out_width), jnp.float32)
    current = b_panel.reshape(k_rows, block_side, out_width)
    for step_number in range(section_total):
        if step_number > 0:
            current = shifted(current, "wide", 1)
        back = (device_column - step_number // section_share) % narrow_count
        row_blocks = lax.dynamic_index_in_dim(held, back, keepdims=False)
        row_blocks = row_blocks[:, step_number % section_share]
        panel_number = (device_row - step_number) % wide_count
        slot_cols = a_cols[:, step_number]
        live_slots = (slot_ids[None, :] < a_counts[:, step_number][:, None]).astype(jnp.float32)
        weights = (
            a_scales[:, step_number]
            * chosen(lax.dynamic_slice(b_scales, (panel_number * k_rows,), (k_rows,)), slot_cols)
            * live_slots
        )
        accumulated = accumulated + section_term(row_blocks, slot_cols, weights, current)
    masked = (
        accumulated.reshape(row_count, block_side, col_blocks, block_side)
        * keep_mask.astype(jnp.float32)[:, None, :, None]
    )
    filtered = masked.astype(jnp.bfloat16).reshape(row_count, block_side, out_width)
    new_order = row_perm[0]
    positions = jnp.arange(row_count, dtype=jnp.int32)
    matches = (new_order[None, :] == positions[:, None]).astype(jnp.int32)
    inverse = jnp.sum(positions[None, :] * matches, axis=1)
    reordered = chosen(filtered, inverse).reshape(row_count * block_side, out_width)
    return lax.all_to_all(reordered, "narrow", split_axis=0, concat_axis=1, tiled=True)


def per_device(*operands):
    wide_count = lax.axis_size("wide")
    narrow_count = lax.axis_size("narrow")
    rows, share, slots, side = operands[0].shape[:4]
    depth, width = operands[4].shape
    fits = rows == 4 and share == 2 and depth == width == 2 * side
    if fits and narrow_count == NARROW and wide_count == WIDE:
        return fused(*operands)
    return by_rings(*operands)


def solution(mesh):
    in_specs = (
        P("wide", "narrow", None, None, None),
        P("wide", None, None),
        P("wide", None, None),
        P("wide", None),
        P("wide", "narrow"),
        P(),
        P("wide", "narrow"),
        P("wide", None),
    )
    out_specs = P(("wide", "narrow"), None)
    return jax.shard_map(
        per_device, mesh=mesh, in_specs=in_specs, out_specs=out_specs, check_vma=False
    )
```

```python
import functools

import jax
import jax.numpy as jnp
from jax import lax
from jax.experimental import pallas as pl
from jax.experimental.pallas import tpu as pltpu
from jax.sharding import PartitionSpec as P

MESH = pl.DeviceIdType.MESH
HALVES = 2
PARTS = 4
LAG = 1
WIDE = 8
DEPTH = 4
NARROW = 4
EARLY = 1


def kernel(
    a_hbm,
    cols_hbm,
    scales_hbm,
    counts_hbm,
    b_hbm,
    b_scales_hbm,
    keep_hbm,
    perm_hbm,
    out,
    cols,
    scales,
    counts,
    b_scales,
    keep,
    perm,
    table_sem,
    a_own,
    left,
    right,
    carry,
    result,
    total,
    load_sem,
    b_recv,
    b_up,
    b_down,
    b_cross,
    k_recv,
    k_down,
    k_mate,
    a_recv,
    a_mate,
    a_far,
    r_send,
    r_recv,
):
    w = lax.axis_index("wide")
    n = lax.axis_index("narrow")
    x = w % 2
    z = w // 2
    y = n // 2
    core = n % 2
    rows, share, slots, side = a_own.shape[:4]
    kb = b_hbm.shape[0] // side
    width = b_hbm.shape[1]
    across = w + 1 - 2 * x
    mate = n + 1 - 2 * core
    far = (n + 2) % 4
    diagonal = 3 - n

    barrier = pltpu.get_barrier_semaphore()
    for peer in ((w, mate), (w, far), (w, diagonal), (across, n)):
        pl.semaphore_signal(barrier, inc=1, device_id=peer, device_id_type=MESH)

    @pl.when(z > 0)
    def _():
        pl.semaphore_signal(barrier, inc=1, device_id=(w - 2, n), device_id_type=MESH)

    @pl.when(z < DEPTH - 1)
    def _():
        pl.semaphore_signal(barrier, inc=1, device_id=(w + 2, n), device_id_type=MESH)

    @pl.when((z == DEPTH - 2) & (core == 1))
    def _():
        pl.semaphore_signal(barrier, inc=1, device_id=(w + 2, mate), device_id_type=MESH)

    @pl.when((z == 0) & (core == 0))
    def _():
        pl.semaphore_signal(barrier, inc=1, device_id=(across, mate), device_id_type=MESH)

    tables = [
        pltpu.make_async_copy(source, kept, table_sem.at[i])
        for i, (source, kept) in enumerate(
            (
                (perm_hbm, perm),
                (cols_hbm, cols),
                (scales_hbm, scales),
                (counts_hbm, counts),
                (b_scales_hbm, b_scales),
                (keep_hbm, keep),
            )
        )
    ]
    for copy in tables:
        copy.start()
    load_a = pltpu.make_async_copy(a_hbm, a_own, load_sem.at[0])
    load_a.start()
    load_b = [
        pltpu.make_async_copy(
            b_hbm.at[t % kb * side : (t % kb + 1) * side, t // kb * side : (t // kb + 1) * side],
            right.at[w * PARTS + t],
            load_sem.at[1 + t],
        )
        for t in range(PARTS)
    ]
    for copy in load_b:
        copy.start()

    def piece(slot, sent, target):
        return pltpu.make_async_remote_copy(
            src_ref=right.at[slot],
            dst_ref=right.at[slot],
            send_sem=sent.at[0],
            recv_sem=b_recv.at[slot],
            device_id=(target, n),
            device_id_type=MESH,
        )

    def upward(slot):
        return piece(slot, b_up, w + 2)

    def downward(slot):
        return piece(slot, b_down, w - 2)

    def crossing(slot):
        return piece(slot, b_cross, across)

    def top_slot(t):
        return (2 * (DEPTH - 1) + x) * PARTS + t

    def lift(t, source, target, sent, landed, wide, narrow):
        return pltpu.make_async_remote_copy(
            src_ref=source,
            dst_ref=target,
            send_sem=sent,
            recv_sem=landed,
            device_id=(wide, narrow),
            device_id_type=MESH,
        )

    def enter(t):
        slot = w * PARTS + t
        return lift(t, right.at[slot], carry.at[t], b_down.at[0], k_recv.at[t], w - 2, mate)

    def carry_down(t):
        return lift(t, carry.at[t], carry.at[t], k_down.at[0], k_recv.at[t], w - 2, n)

    def carry_mate(t):
        slot = top_slot(t)
        return lift(t, carry.at[t], right.at[slot], k_mate.at[0], b_recv.at[slot], w, mate)

    def carry_cross(t):
        slot = top_slot(t)
        return lift(t, carry.at[t], right.at[slot], k_down.at[0], b_recv.at[slot], across, mate)

    def block(origin, pair, j, sent, target):
        return pltpu.make_async_remote_copy(
            src_ref=left.at[origin, pair, j],
            dst_ref=left.at[origin, pair, j],
            send_sem=sent,
            recv_sem=a_recv.at[origin, pair, j],
            device_id=(w, target),
            device_id_type=MESH,
        )

    def to_far(pair, j):
        return block(n, pair, j, a_far.at[0], far)

    def to_mate(pair, j):
        return block(n, pair, j, a_mate.at[0], mate)

    def from_far(pair, j):
        return block(far, pair, j, a_far.at[0], far)

    def pass_on(pair, j):
        return block(far, pair, j, a_mate.at[1], mate)

    def home(q):
        found = jnp.int32(0)
        for r in range(rows):
            found = jnp.where(perm[0, r] == q, r, found)
        return found

    def scale(pair, j):
        s = n * share + j
        panel = (w - s + WIDE) % WIDE
        for c in range(2):
            r = home(2 * pair + c)
            weights, places = [], []
            for m in range(slots):
                place = cols[r, m, s]
                live = jnp.where(m < counts[r, s], 1.0, 0.0)
                weights.append(scales[r, m, s] * b_scales[panel * kb + place] * live)
                places.append(place)
            for k in range(kb):
                value = None
                for m in range(slots):
                    weight = jnp.where(places[m] == k, weights[m], 0.0)
                    term = a_own[r, j, m].astype(jnp.float32) * weight
                    value = term if value is None else value + term
                left[n, pair, j, c * side : (c + 1) * side, k * side : (k + 1) * side] = (
                    value.astype(jnp.bfloat16)
                )

    pairs = (y, 1 - y)
    units = [(pair, j) for pair in pairs for j in range(share)]
    for copy in tables:
        copy.wait()
    load_a.wait()
    for unit in units[:EARLY]:
        scale(*unit)
    for copy in load_b:
        copy.wait()

    neighbours = jnp.where(z > 0, 1, 0) + jnp.where(z < DEPTH - 1, 1, 0)
    lifted = ((z == DEPTH - 1) & (core == 0)) | ((z == 0) & (core == 1))
    pl.semaphore_wait(barrier, 4 + neighbours + jnp.where(lifted, 1, 0))

    @pl.when((z == DEPTH - 1) & (core == 0))
    def _():
        for t in range(PARTS):
            enter(t).start()

    @pl.when((z == DEPTH - 1) & (core == 1))
    def _():
        for t in range(PARTS):
            downward(w * PARTS + t).start()

    for unit in units[:EARLY]:
        to_far(*unit).start()
    for t in range(PARTS):
        own = w * PARTS + t

        @pl.when(z < DEPTH - 1)
        def _():
            upward(own).start()

        @pl.when((z > 0) & (z < DEPTH - 1))
        def _():
            downward(own).start()

        crossing(own).start()

    for unit in units[:EARLY]:
        to_mate(*unit).start()
    for unit in units[EARLY:]:
        scale(*unit)
        to_far(*unit).start()
        to_mate(*unit).start()

    def relay(step, t):
        from_below = (w - 2 * step) * PARTS + t
        from_above = (w + 2 * step) * PARTS + t

        @pl.when(z - step >= 0)
        def _():
            upward(from_below).wait_recv()

            @pl.when(z < DEPTH - 1)
            def _():
                upward(from_below).start()

            crossing(from_below).start()

        @pl.when(z + step < DEPTH)
        def _():
            downward(from_above).wait_recv()

            @pl.when((z > 0) & ((z + step < DEPTH - 1) | (core == 1)))
            def _():
                downward(from_above).start()

            @pl.when((z > 0) | (step < DEPTH - 1) | (core == 1))
            def _():
                crossing(from_above).start()

    def ferry(step, t):
        @pl.when((z + step == DEPTH - 1) & (core == 1))
        def _():
            carry_down(t).wait_recv()
            if step < DEPTH - 1:
                carry_down(t).start()
            else:
                carry_cross(t).start()
            carry_mate(t).start()

    def hand_over(pair, j):
        from_far(pair, j).wait_recv()
        pass_on(pair, j).start()

    def mate_arrived(pair, j):
        block(mate, pair, j, a_mate.at[0], mate).wait_recv()

    def diagonal_arrived(pair, j):
        block(diagonal, pair, j, a_mate.at[1], mate).wait_recv()

    near = (
        z,
        jnp.where(z == 0, 1, z - 1),
        jnp.where(z == 0, 2, jnp.where(z == 3, 1, z + 1)),
        jnp.where(z < 2, 3, 0),
    )

    def peer_arrived(level, h):
        for t in range(h * kb, h * kb + kb):
            crossing((2 * level + 1 - x) * PARTS + t).wait_recv()

    def half(panel, h):
        return right[pl.ds(panel * PARTS + h * kb, kb)].reshape(kb * side, side)

    def term(pair, j, level, h):
        panel = 2 * level + (x if j == 0 else 1 - x)
        origin = ((w - panel + WIDE) % WIDE) // share
        if h is None:
            tile = jnp.concatenate([half(panel, i) for i in range(HALVES)], axis=1)
        else:
            tile = half(panel, h)
        return jnp.dot(left[origin, pair, j], tile, preferred_element_type=jnp.float32)

    def add(slot, pair, terms, first=False):
        value = None
        for j, level in terms:
            product = term(pair, j, near[level], None)
            value = product if value is None else value + product
        total[slot] = value if first else total[slot] + value

    give, hold = 1 - y, y

    def deliver(c, h, source, target):
        start = pl.multiple_of(n * width + h * side, side)
        return pltpu.make_async_remote_copy(
            src_ref=result.at[source, c, h],
            dst_ref=out.at[:, pl.ds(start, side)],
            send_sem=r_send.at[source],
            recv_sem=r_recv.at[n, h],
            device_id=(w, target),
            device_id_type=MESH,
        )

    for t in range(PARTS):
        relay(1, t)
        if t >= LAG:
            ferry(1, t - LAG)
    for t in range(PARTS - LAG, PARTS):
        ferry(1, t)
    hand_over(give, 0)
    for t in range(PARTS):
        ferry(2, t)
        relay(2, t)
        if t == 1:
            hand_over(give, 1)
    mate_arrived(give, 0)
    mate_arrived(give, 1)
    diagonal_arrived(give, 0)
    add(0, give, [(0, 0), (0, 1), (0, 2)], first=True)
    for t in range(PARTS // 2):
        ferry(3, t)
        relay(3, t)
    diagonal_arrived(give, 1)
    for level in range(2):
        for h in range(HALVES):
            peer_arrived(near[level], h)
    add(0, give, [(1, 0), (1, 1)])
    hand_over(hold, 0)
    for t in range(PARTS // 2, PARTS):
        ferry(3, t)
        relay(3, t)
    for h in range(HALVES):
        if h == 1:
            hand_over(hold, 1)
        peer_arrived(near[2], h)
        value = total[0, :, h * side : (h + 1) * side] + term(give, 0, near[3], h)
        value = value + term(give, 1, near[2], h)
        peer_arrived(near[3], h)
        value = value + term(give, 1, near[3], h)
        for c in range(2):
            q = 2 * give + c
            kept = value[c * side : (c + 1) * side] * keep[h, home(q)].astype(jnp.float32)
            result[0, c, h] = kept.astype(jnp.bfloat16)
            deliver(c, h, 0, q).start()
    mate_arrived(hold, 0)
    mate_arrived(hold, 1)
    diagonal_arrived(hold, 0)
    add(1, hold, [(0, 0), (0, 1), (0, 2), (0, 3)], first=True)
    diagonal_arrived(hold, 1)
    add(1, hold, [(1, 0), (1, 1), (1, 2), (1, 3)])
    for h in range(HALVES):
        c = 1 - core
        kept = total[1, pl.ds(pl.multiple_of(c * side, side), side), h * side : (h + 1) * side]
        result[1, 0, h] = (kept * keep[h, home(mate)].astype(jnp.float32)).astype(jnp.bfloat16)
        deliver(0, h, 1, mate).start()
    for h in range(HALVES):
        kept = total[1, pl.ds(pl.multiple_of(core * side, side), side), h * side : (h + 1) * side]
        start = pl.multiple_of(n * width + h * side, side)
        out[:, pl.ds(start, side)] = (kept * keep[h, home(n)].astype(jnp.float32)).astype(
            jnp.bfloat16
        )

    def drain(source, sem):
        pltpu.make_async_remote_copy(
            src_ref=source,
            dst_ref=source,
            send_sem=sem,
            recv_sem=b_recv.at[0],
            device_id=(w, mate),
            device_id_type=MESH,
        ).wait_send()

    for sem in (a_far.at[0], a_mate.at[0], a_mate.at[1]):
        drain(left.at[n], sem)
    for k in range(DEPTH):
        for c in range(2):

            @pl.when((z == k) & (core == c))
            def _(k=k, c=c):
                if k < DEPTH - 1:
                    drain(right.at[pl.ds(0, PARTS * (k + 1))], b_up.at[0])
                if k > 0:
                    levels = DEPTH - k if c == 1 else max(DEPTH - 1 - k, 1)
                    drain(right.at[pl.ds(0, PARTS * levels)], b_down.at[0])
                levels = DEPTH if c == 1 or k > 0 else DEPTH - 1
                drain(right.at[pl.ds(0, PARTS * levels)], b_cross.at[0])
                if c == 1 and k < DEPTH - 1:
                    drain(right.at[pl.ds(0, PARTS)], k_down.at[0])
                    drain(right.at[pl.ds(0, PARTS)], k_mate.at[0])

    drain(result.at[0], r_send.at[0])
    drain(result.at[1, 0], r_send.at[1])
    for origin in (mate, far, diagonal):
        for h in range(HALVES):
            start = pl.multiple_of(origin * width + h * side, side)
            pltpu.make_async_remote_copy(
                src_ref=result.at[0, 0, h],
                dst_ref=out.at[:, pl.ds(start, side)],
                send_sem=r_send.at[0],
                recv_sem=r_recv.at[origin, h],
                device_id=(w, origin),
                device_id_type=MESH,
            ).wait_recv()


def fused(a_blocks, a_cols, a_scales, a_counts, b_panel, b_scales, keep_mask, row_perm):
    rows, share, slots, side = a_blocks.shape[:4]
    depth, width = b_panel.shape
    pieces = WIDE * PARTS
    in_place = pl.BlockSpec(memory_space=pltpu.HBM)
    dma = pltpu.SemaphoreType.DMA
    return pl.pallas_call(
        kernel,
        out_shape=pltpu.VMEM((side, width * NARROW), jnp.bfloat16),
        in_specs=[in_place] * 8,
        out_specs=pl.BlockSpec(memory_space=pltpu.VMEM),
        scratch_shapes=[
            pltpu.SMEM((rows, slots, a_cols.shape[1]), jnp.int32),
            pltpu.SMEM((rows, slots, a_cols.shape[1]), jnp.float32),
            pltpu.SMEM(a_counts.shape, jnp.int32),
            pltpu.SMEM(b_scales.shape, jnp.float32),
            pltpu.SMEM((keep_mask.shape[1], rows), jnp.int32),
            pltpu.SMEM(row_perm.shape, jnp.int32),
            dma((6,)),
            pltpu.VMEM(a_blocks.shape, jnp.bfloat16),
            pltpu.VMEM((NARROW, 2, share, 2 * side, depth), jnp.bfloat16),
            pltpu.VMEM((pieces, side, side), jnp.bfloat16),
            pltpu.VMEM((PARTS, side, side), jnp.bfloat16),
            pltpu.VMEM((2, 2, HALVES, side, side), jnp.bfloat16),
            pltpu.VMEM((2, 2 * side, width), jnp.float32),
            dma((1 + PARTS,)),
            dma((pieces,)),
            dma((1,)),
            dma((1,)),
            dma((1,)),
            dma((PARTS,)),
            dma((1,)),
            dma((1,)),
            dma((NARROW, 2, share)),
            dma((2,)),
            dma((1,)),
            dma((2,)),
            dma((NARROW, HALVES)),
        ],
        compiler_params=pltpu.CompilerParams(
            collective_id=0, has_side_effects=True, vmem_limit_bytes=60 * 2**20
        ),
    )(
        a_blocks,
        jnp.transpose(a_cols, (0, 2, 1)),
        jnp.transpose(a_scales, (0, 2, 1)),
        a_counts,
        b_panel,
        b_scales,
        jnp.transpose(keep_mask),
        row_perm,
    )


def shifted(block, axis, distance):
    devices = range(lax.axis_size(axis))
    route = [((i - distance) % len(devices), i) for i in devices]
    return lax.ppermute(block, axis, route)


def chosen(table, index):
    tail = (1,) * (table.ndim - 1)
    index = index.reshape(index.shape + tail)
    found = jnp.broadcast_to(table[0], index.shape[: index.ndim - len(tail)] + table.shape[1:])
    for k in range(1, table.shape[0]):
        found = jnp.where(index == k, table[k], found)
    return found


def section_term(row_blocks, slot_cols, weights, b_tiles):
    row_count = row_blocks.shape[0]
    slot_count = row_blocks.shape[1]
    block_side = row_blocks.shape[2]
    scaled = (row_blocks.astype(jnp.float32) * weights[:, :, None, None]).astype(jnp.bfloat16)
    left = jnp.transpose(scaled, (0, 2, 1, 3)).reshape(
        row_count, block_side, slot_count * block_side
    )
    right = chosen(b_tiles, slot_cols.reshape(-1)).reshape(
        row_count, slot_count * block_side, b_tiles.shape[2]
    )
    return jnp.einsum("rik,rkj->rij", left, right, preferred_element_type=jnp.float32)


def by_rings(a_blocks, a_cols, a_scales, a_counts, b_panel, b_scales, keep_mask, row_perm):
    wide_count = lax.axis_size("wide")
    narrow_count = lax.axis_size("narrow")
    device_row = lax.axis_index("wide")
    device_column = lax.axis_index("narrow")
    row_count, section_share, slot_count, block_side = a_blocks.shape[:4]
    section_total = section_share * narrow_count
    k_rows = b_panel.shape[0] // block_side
    out_width = b_panel.shape[1]
    col_blocks = out_width // block_side
    held = [a_blocks]
    for _ in range(narrow_count - 1):
        held.append(shifted(held[-1], "narrow", 1))
    held = jnp.stack(held)
    slot_ids = jnp.arange(slot_count, dtype=jnp.int32)
    accumulated = jnp.zeros((row_count, block_side, out_width), jnp.float32)
    current = b_panel.reshape(k_rows, block_side, out_width)
    for step_number in range(section_total):
        if step_number > 0:
            current = shifted(current, "wide", 1)
        back = (device_column - step_number // section_share) % narrow_count
        row_blocks = lax.dynamic_index_in_dim(held, back, keepdims=False)
        row_blocks = row_blocks[:, step_number % section_share]
        panel_number = (device_row - step_number) % wide_count
        slot_cols = a_cols[:, step_number]
        live_slots = (slot_ids[None, :] < a_counts[:, step_number][:, None]).astype(jnp.float32)
        weights = (
            a_scales[:, step_number]
            * chosen(lax.dynamic_slice(b_scales, (panel_number * k_rows,), (k_rows,)), slot_cols)
            * live_slots
        )
        accumulated = accumulated + section_term(row_blocks, slot_cols, weights, current)
    masked = (
        accumulated.reshape(row_count, block_side, col_blocks, block_side)
        * keep_mask.astype(jnp.float32)[:, None, :, None]
    )
    filtered = masked.astype(jnp.bfloat16).reshape(row_count, block_side, out_width)
    new_order = row_perm[0]
    positions = jnp.arange(row_count, dtype=jnp.int32)
    matches = (new_order[None, :] == positions[:, None]).astype(jnp.int32)
    inverse = jnp.sum(positions[None, :] * matches, axis=1)
    reordered = chosen(filtered, inverse).reshape(row_count * block_side, out_width)
    return lax.all_to_all(reordered, "narrow", split_axis=0, concat_axis=1, tiled=True)


def per_device(*operands):
    wide_count = lax.axis_size("wide")
    narrow_count = lax.axis_size("narrow")
    rows, share, slots, side = operands[0].shape[:4]
    depth, width = operands[4].shape
    fits = rows == 4 and share == 2 and depth == width == 2 * side
    if fits and narrow_count == NARROW and wide_count == WIDE:
        return fused(*operands)
    return by_rings(*operands)


def solution(mesh):
    in_specs = (
        P("wide", "narrow", None, None, None),
        P("wide", None, None),
        P("wide", None, None),
        P("wide", None),
        P("wide", "narrow"),
        P(),
        P("wide", "narrow"),
        P("wide", None),
    )
    out_specs = P(("wide", "narrow"), None)
    return jax.shard_map(
        per_device, mesh=mesh, in_specs=in_specs, out_specs=out_specs, check_vma=False
    )
```

```python
import functools

import jax
import jax.numpy as jnp
from jax import lax
from jax.experimental import pallas as pl
from jax.experimental.pallas import tpu as pltpu
from jax.sharding import PartitionSpec as P

MESH = pl.DeviceIdType.MESH
HALVES = 2
PARTS = 4
LAG = 1
WIDE = 8
DEPTH = 4
NARROW = 4
EARLY = 1


def kernel(
    a_hbm,
    cols_hbm,
    scales_hbm,
    counts_hbm,
    b_hbm,
    b_scales_hbm,
    keep_hbm,
    perm_hbm,
    out,
    cols,
    scales,
    counts,
    b_scales,
    keep,
    perm,
    table_sem,
    a_own,
    left,
    right,
    carry,
    result,
    total,
    load_sem,
    b_recv,
    b_up,
    b_down,
    b_cross,
    k_recv,
    k_down,
    k_mate,
    a_recv,
    a_mate,
    a_far,
    r_send,
    r_recv,
):
    w = lax.axis_index("wide")
    n = lax.axis_index("narrow")
    x = w % 2
    z = w // 2
    y = n // 2
    core = n % 2
    rows, share, slots, side = a_own.shape[:4]
    kb = b_hbm.shape[0] // side
    width = b_hbm.shape[1]
    across = w + 1 - 2 * x
    mate = n + 1 - 2 * core
    far = (n + 2) % 4
    diagonal = 3 - n

    barrier = pltpu.get_barrier_semaphore()
    for peer in ((w, mate), (w, far), (w, diagonal), (across, n)):
        pl.semaphore_signal(barrier, inc=1, device_id=peer, device_id_type=MESH)

    @pl.when(z > 0)
    def _():
        pl.semaphore_signal(barrier, inc=1, device_id=(w - 2, n), device_id_type=MESH)

    @pl.when(z < DEPTH - 1)
    def _():
        pl.semaphore_signal(barrier, inc=1, device_id=(w + 2, n), device_id_type=MESH)

    @pl.when((z == DEPTH - 2) & (core == 1))
    def _():
        pl.semaphore_signal(barrier, inc=1, device_id=(w + 2, mate), device_id_type=MESH)

    @pl.when((z == 0) & (core == 0))
    def _():
        pl.semaphore_signal(barrier, inc=1, device_id=(across, mate), device_id_type=MESH)

    tables = [
        pltpu.make_async_copy(source, kept, table_sem.at[i])
        for i, (source, kept) in enumerate(
            (
                (perm_hbm, perm),
                (cols_hbm, cols),
                (scales_hbm, scales),
                (counts_hbm, counts),
                (b_scales_hbm, b_scales),
                (keep_hbm, keep),
            )
        )
    ]
    for copy in tables:
        copy.start()
    load_a = pltpu.make_async_copy(a_hbm, a_own, load_sem.at[0])
    load_a.start()
    load_b = [
        pltpu.make_async_copy(
            b_hbm.at[t % kb * side : (t % kb + 1) * side, t // kb * side : (t // kb + 1) * side],
            right.at[w * PARTS + t],
            load_sem.at[1 + t],
        )
        for t in range(PARTS)
    ]
    for copy in load_b:
        copy.start()

    def piece(slot, sent, target):
        return pltpu.make_async_remote_copy(
            src_ref=right.at[slot],
            dst_ref=right.at[slot],
            send_sem=sent.at[0],
            recv_sem=b_recv.at[slot],
            device_id=(target, n),
            device_id_type=MESH,
        )

    def upward(slot):
        return piece(slot, b_up, w + 2)

    def downward(slot):
        return piece(slot, b_down, w - 2)

    def crossing(slot):
        return piece(slot, b_cross, across)

    def top_slot(t):
        return (2 * (DEPTH - 1) + x) * PARTS + t

    def lift(t, source, target, sent, landed, wide, narrow):
        return pltpu.make_async_remote_copy(
            src_ref=source,
            dst_ref=target,
            send_sem=sent,
            recv_sem=landed,
            device_id=(wide, narrow),
            device_id_type=MESH,
        )

    def enter(t):
        slot = w * PARTS + t
        return lift(t, right.at[slot], carry.at[t], b_down.at[0], k_recv.at[t], w - 2, mate)

    def carry_down(t):
        return lift(t, carry.at[t], carry.at[t], k_down.at[0], k_recv.at[t], w - 2, n)

    def carry_mate(t):
        slot = top_slot(t)
        return lift(t, carry.at[t], right.at[slot], k_mate.at[0], b_recv.at[slot], w, mate)

    def carry_cross(t):
        slot = top_slot(t)
        return lift(t, carry.at[t], right.at[slot], k_down.at[0], b_recv.at[slot], across, mate)

    def block(origin, pair, j, sent, target):
        return pltpu.make_async_remote_copy(
            src_ref=left.at[origin, pair, j],
            dst_ref=left.at[origin, pair, j],
            send_sem=sent,
            recv_sem=a_recv.at[origin, pair, j],
            device_id=(w, target),
            device_id_type=MESH,
        )

    def to_far(pair, j):
        return block(n, pair, j, a_far.at[0], far)

    def to_mate(pair, j):
        return block(n, pair, j, a_mate.at[0], mate)

    def from_far(pair, j):
        return block(far, pair, j, a_far.at[0], far)

    def pass_on(pair, j):
        return block(far, pair, j, a_mate.at[1], mate)

    def home(q):
        found = jnp.int32(0)
        for r in range(rows):
            found = jnp.where(perm[0, r] == q, r, found)
        return found

    def scale(pair, j):
        s = n * share + j
        panel = (w - s + WIDE) % WIDE
        for c in range(2):
            r = home(2 * pair + c)
            weights, places = [], []
            for m in range(slots):
                place = cols[r, m, s]
                live = jnp.where(m < counts[r, s], 1.0, 0.0)
                weights.append(scales[r, m, s] * b_scales[panel * kb + place] * live)
                places.append(place)
            for k in range(kb):
                value = None
                for m in range(slots):
                    weight = jnp.where(places[m] == k, weights[m], 0.0)
                    term = a_own[r, j, m].astype(jnp.float32) * weight
                    value = term if value is None else value + term
                left[n, pair, j, c * side : (c + 1) * side, k * side : (k + 1) * side] = (
                    value.astype(jnp.bfloat16)
                )

    pairs = (y, 1 - y)
    units = [(pair, j) for pair in pairs for j in range(share)]
    for copy in tables:
        copy.wait()
    load_a.wait()
    for unit in units[:EARLY]:
        scale(*unit)
    for copy in load_b:
        copy.wait()

    neighbours = jnp.where(z > 0, 1, 0) + jnp.where(z < DEPTH - 1, 1, 0)
    lifted = ((z == DEPTH - 1) & (core == 0)) | ((z == 0) & (core == 1))
    pl.semaphore_wait(barrier, 4 + neighbours + jnp.where(lifted, 1, 0))

    @pl.when((z == DEPTH - 1) & (core == 0))
    def _():
        for t in range(PARTS):
            enter(t).start()

    @pl.when((z == DEPTH - 1) & (core == 1))
    def _():
        for t in range(PARTS):
            downward(w * PARTS + t).start()

    for unit in units[:EARLY]:
        to_far(*unit).start()
    for t in range(PARTS):
        own = w * PARTS + t

        @pl.when(z < DEPTH - 1)
        def _():
            upward(own).start()

        @pl.when((z > 0) & (z < DEPTH - 1))
        def _():
            downward(own).start()

        crossing(own).start()

    for unit in units[:EARLY]:
        to_mate(*unit).start()
    for unit in units[EARLY:]:
        scale(*unit)
        to_far(*unit).start()
        to_mate(*unit).start()

    def relay(step, t):
        from_below = (w - 2 * step) * PARTS + t
        from_above = (w + 2 * step) * PARTS + t

        @pl.when(z - step >= 0)
        def _():
            upward(from_below).wait_recv()

            @pl.when(z < DEPTH - 1)
            def _():
                upward(from_below).start()

            crossing(from_below).start()

        @pl.when(z + step < DEPTH)
        def _():
            downward(from_above).wait_recv()

            @pl.when((z > 0) & ((z + step < DEPTH - 1) | (core == 1)))
            def _():
                downward(from_above).start()

            @pl.when((z > 0) | (step < DEPTH - 1) | (core == 1))
            def _():
                crossing(from_above).start()

    def ferry(step, t):
        @pl.when((z + step == DEPTH - 1) & (core == 1))
        def _():
            carry_down(t).wait_recv()
            if step < DEPTH - 1:
                carry_down(t).start()
            else:
                carry_cross(t).start()
            carry_mate(t).start()

    def hand_over(pair, j):
        from_far(pair, j).wait_recv()
        pass_on(pair, j).start()

    def mate_arrived(pair, j):
        block(mate, pair, j, a_mate.at[0], mate).wait_recv()

    def diagonal_arrived(pair, j):
        block(diagonal, pair, j, a_mate.at[1], mate).wait_recv()

    near = (
        z,
        jnp.where(z == 0, 1, z - 1),
        jnp.where(z == 0, 2, jnp.where(z == 3, 1, z + 1)),
        jnp.where(z < 2, 3, 0),
    )

    def peer_arrived(level, h):
        for t in range(h * kb, h * kb + kb):
            crossing((2 * level + 1 - x) * PARTS + t).wait_recv()

    def half(panel, h):
        return right[pl.ds(panel * PARTS + h * kb, kb)].reshape(kb * side, side)

    def term(pair, j, level, h):
        panel = 2 * level + (x if j == 0 else 1 - x)
        origin = ((w - panel + WIDE) % WIDE) // share
        if h is None:
            tile = jnp.concatenate([half(panel, i) for i in range(HALVES)], axis=1)
        else:
            tile = half(panel, h)
        return jnp.dot(left[origin, pair, j], tile, preferred_element_type=jnp.float32)

    def add(slot, pair, terms, first=False):
        value = None
        for j, level in terms:
            product = term(pair, j, near[level], None)
            value = product if value is None else value + product
        total[slot] = value if first else total[slot] + value

    give, hold = 1 - y, y

    def deliver(c, h, source, target):
        start = pl.multiple_of(n * width + h * side, side)
        return pltpu.make_async_remote_copy(
            src_ref=result.at[source, c, h],
            dst_ref=out.at[:, pl.ds(start, side)],
            send_sem=r_send.at[source],
            recv_sem=r_recv.at[n, h],
            device_id=(w, target),
            device_id_type=MESH,
        )

    for t in range(PARTS):
        relay(1, t)
        if t >= LAG:
            ferry(1, t - LAG)
    for t in range(PARTS - LAG, PARTS):
        ferry(1, t)
    hand_over(give, 0)
    for t in range(PARTS):
        ferry(2, t)
        relay(2, t)
        if t == 1:
            hand_over(give, 1)
    mate_arrived(give, 0)
    mate_arrived(give, 1)
    diagonal_arrived(give, 0)
    add(0, give, [(0, 0), (0, 1), (0, 2)], first=True)
    for t in range(PARTS // 2):
        ferry(3, t)
        relay(3, t)
    diagonal_arrived(give, 1)
    for level in range(2):
        for h in range(HALVES):
            peer_arrived(near[level], h)
    add(0, give, [(1, 0), (1, 1)])
    hand_over(hold, 0)
    for t in range(PARTS // 2, PARTS):
        ferry(3, t)
        relay(3, t)
    for h in range(HALVES):
        peer_arrived(near[2], h)
        value = total[0, :, h * side : (h + 1) * side] + term(give, 0, near[3], h)
        value = value + term(give, 1, near[2], h)
        peer_arrived(near[3], h)
        value = value + term(give, 1, near[3], h)
        for c in range(2):
            q = 2 * give + c
            kept = value[c * side : (c + 1) * side] * keep[h, home(q)].astype(jnp.float32)
            result[0, c, h] = kept.astype(jnp.bfloat16)
            deliver(c, h, 0, q).start()
    hand_over(hold, 1)
    mate_arrived(hold, 0)
    mate_arrived(hold, 1)
    diagonal_arrived(hold, 0)
    add(1, hold, [(0, 0), (0, 1), (0, 2), (0, 3)], first=True)
    diagonal_arrived(hold, 1)
    add(1, hold, [(1, 0), (1, 1), (1, 2), (1, 3)])
    for h in range(HALVES):
        c = 1 - core
        kept = total[1, pl.ds(pl.multiple_of(c * side, side), side), h * side : (h + 1) * side]
        result[1, 0, h] = (kept * keep[h, home(mate)].astype(jnp.float32)).astype(jnp.bfloat16)
        deliver(0, h, 1, mate).start()
    for h in range(HALVES):
        kept = total[1, pl.ds(pl.multiple_of(core * side, side), side), h * side : (h + 1) * side]
        start = pl.multiple_of(n * width + h * side, side)
        out[:, pl.ds(start, side)] = (kept * keep[h, home(n)].astype(jnp.float32)).astype(
            jnp.bfloat16
        )

    def drain(source, sem):
        pltpu.make_async_remote_copy(
            src_ref=source,
            dst_ref=source,
            send_sem=sem,
            recv_sem=b_recv.at[0],
            device_id=(w, mate),
            device_id_type=MESH,
        ).wait_send()

    for sem in (a_far.at[0], a_mate.at[0], a_mate.at[1]):
        drain(left.at[n], sem)
    for k in range(DEPTH):
        for c in range(2):

            @pl.when((z == k) & (core == c))
            def _(k=k, c=c):
                if k < DEPTH - 1:
                    drain(right.at[pl.ds(0, PARTS * (k + 1))], b_up.at[0])
                if k > 0:
                    levels = DEPTH - k if c == 1 else max(DEPTH - 1 - k, 1)
                    drain(right.at[pl.ds(0, PARTS * levels)], b_down.at[0])
                levels = DEPTH if c == 1 or k > 0 else DEPTH - 1
                drain(right.at[pl.ds(0, PARTS * levels)], b_cross.at[0])
                if c == 1 and k < DEPTH - 1:
                    drain(right.at[pl.ds(0, PARTS)], k_down.at[0])
                    drain(right.at[pl.ds(0, PARTS)], k_mate.at[0])

    drain(result.at[0], r_send.at[0])
    drain(result.at[1, 0], r_send.at[1])
    for origin in (mate, far, diagonal):
        for h in range(HALVES):
            start = pl.multiple_of(origin * width + h * side, side)
            pltpu.make_async_remote_copy(
                src_ref=result.at[0, 0, h],
                dst_ref=out.at[:, pl.ds(start, side)],
                send_sem=r_send.at[0],
                recv_sem=r_recv.at[origin, h],
                device_id=(w, origin),
                device_id_type=MESH,
            ).wait_recv()


def fused(a_blocks, a_cols, a_scales, a_counts, b_panel, b_scales, keep_mask, row_perm):
    rows, share, slots, side = a_blocks.shape[:4]
    depth, width = b_panel.shape
    pieces = WIDE * PARTS
    in_place = pl.BlockSpec(memory_space=pltpu.HBM)
    dma = pltpu.SemaphoreType.DMA
    return pl.pallas_call(
        kernel,
        out_shape=pltpu.VMEM((side, width * NARROW), jnp.bfloat16),
        in_specs=[in_place] * 8,
        out_specs=pl.BlockSpec(memory_space=pltpu.VMEM),
        scratch_shapes=[
            pltpu.SMEM((rows, slots, a_cols.shape[1]), jnp.int32),
            pltpu.SMEM((rows, slots, a_cols.shape[1]), jnp.float32),
            pltpu.SMEM(a_counts.shape, jnp.int32),
            pltpu.SMEM(b_scales.shape, jnp.float32),
            pltpu.SMEM((keep_mask.shape[1], rows), jnp.int32),
            pltpu.SMEM(row_perm.shape, jnp.int32),
            dma((6,)),
            pltpu.VMEM(a_blocks.shape, jnp.bfloat16),
            pltpu.VMEM((NARROW, 2, share, 2 * side, depth), jnp.bfloat16),
            pltpu.VMEM((pieces, side, side), jnp.bfloat16),
            pltpu.VMEM((PARTS, side, side), jnp.bfloat16),
            pltpu.VMEM((2, 2, HALVES, side, side), jnp.bfloat16),
            pltpu.VMEM((2, 2 * side, width), jnp.float32),
            dma((1 + PARTS,)),
            dma((pieces,)),
            dma((1,)),
            dma((1,)),
            dma((1,)),
            dma((PARTS,)),
            dma((1,)),
            dma((1,)),
            dma((NARROW, 2, share)),
            dma((2,)),
            dma((1,)),
            dma((2,)),
            dma((NARROW, HALVES)),
        ],
        compiler_params=pltpu.CompilerParams(
            collective_id=0, has_side_effects=True, vmem_limit_bytes=60 * 2**20
        ),
    )(
        a_blocks,
        jnp.transpose(a_cols, (0, 2, 1)),
        jnp.transpose(a_scales, (0, 2, 1)),
        a_counts,
        b_panel,
        b_scales,
        jnp.transpose(keep_mask),
        row_perm,
    )


def shifted(block, axis, distance):
    devices = range(lax.axis_size(axis))
    route = [((i - distance) % len(devices), i) for i in devices]
    return lax.ppermute(block, axis, route)


def chosen(table, index):
    tail = (1,) * (table.ndim - 1)
    index = index.reshape(index.shape + tail)
    found = jnp.broadcast_to(table[0], index.shape[: index.ndim - len(tail)] + table.shape[1:])
    for k in range(1, table.shape[0]):
        found = jnp.where(index == k, table[k], found)
    return found


def section_term(row_blocks, slot_cols, weights, b_tiles):
    row_count = row_blocks.shape[0]
    slot_count = row_blocks.shape[1]
    block_side = row_blocks.shape[2]
    scaled = (row_blocks.astype(jnp.float32) * weights[:, :, None, None]).astype(jnp.bfloat16)
    left = jnp.transpose(scaled, (0, 2, 1, 3)).reshape(
        row_count, block_side, slot_count * block_side
    )
    right = chosen(b_tiles, slot_cols.reshape(-1)).reshape(
        row_count, slot_count * block_side, b_tiles.shape[2]
    )
    return jnp.einsum("rik,rkj->rij", left, right, preferred_element_type=jnp.float32)


def by_rings(a_blocks, a_cols, a_scales, a_counts, b_panel, b_scales, keep_mask, row_perm):
    wide_count = lax.axis_size("wide")
    narrow_count = lax.axis_size("narrow")
    device_row = lax.axis_index("wide")
    device_column = lax.axis_index("narrow")
    row_count, section_share, slot_count, block_side = a_blocks.shape[:4]
    section_total = section_share * narrow_count
    k_rows = b_panel.shape[0] // block_side
    out_width = b_panel.shape[1]
    col_blocks = out_width // block_side
    held = [a_blocks]
    for _ in range(narrow_count - 1):
        held.append(shifted(held[-1], "narrow", 1))
    held = jnp.stack(held)
    slot_ids = jnp.arange(slot_count, dtype=jnp.int32)
    accumulated = jnp.zeros((row_count, block_side, out_width), jnp.float32)
    current = b_panel.reshape(k_rows, block_side, out_width)
    for step_number in range(section_total):
        if step_number > 0:
            current = shifted(current, "wide", 1)
        back = (device_column - step_number // section_share) % narrow_count
        row_blocks = lax.dynamic_index_in_dim(held, back, keepdims=False)
        row_blocks = row_blocks[:, step_number % section_share]
        panel_number = (device_row - step_number) % wide_count
        slot_cols = a_cols[:, step_number]
        live_slots = (slot_ids[None, :] < a_counts[:, step_number][:, None]).astype(jnp.float32)
        weights = (
            a_scales[:, step_number]
            * chosen(lax.dynamic_slice(b_scales, (panel_number * k_rows,), (k_rows,)), slot_cols)
            * live_slots
        )
        accumulated = accumulated + section_term(row_blocks, slot_cols, weights, current)
    masked = (
        accumulated.reshape(row_count, block_side, col_blocks, block_side)
        * keep_mask.astype(jnp.float32)[:, None, :, None]
    )
    filtered = masked.astype(jnp.bfloat16).reshape(row_count, block_side, out_width)
    new_order = row_perm[0]
    positions = jnp.arange(row_count, dtype=jnp.int32)
    matches = (new_order[None, :] == positions[:, None]).astype(jnp.int32)
    inverse = jnp.sum(positions[None, :] * matches, axis=1)
    reordered = chosen(filtered, inverse).reshape(row_count * block_side, out_width)
    return lax.all_to_all(reordered, "narrow", split_axis=0, concat_axis=1, tiled=True)


def per_device(*operands):
    wide_count = lax.axis_size("wide")
    narrow_count = lax.axis_size("narrow")
    rows, share, slots, side = operands[0].shape[:4]
    depth, width = operands[4].shape
    fits = rows == 4 and share == 2 and depth == width == 2 * side
    if fits and narrow_count == NARROW and wide_count == WIDE:
        return fused(*operands)
    return by_rings(*operands)


def solution(mesh):
    in_specs = (
        P("wide", "narrow", None, None, None),
        P("wide", None, None),
        P("wide", None, None),
        P("wide", None),
        P("wide", "narrow"),
        P(),
        P("wide", "narrow"),
        P("wide", None),
    )
    out_specs = P(("wide", "narrow"), None)
    return jax.shard_map(
        per_device, mesh=mesh, in_specs=in_specs, out_specs=out_specs, check_vma=False
    )
```

```python
import functools

import jax
import jax.numpy as jnp
from jax import lax
from jax.experimental import pallas as pl
from jax.experimental.pallas import tpu as pltpu
from jax.sharding import PartitionSpec as P

MESH = pl.DeviceIdType.MESH
HALVES = 2
PARTS = 4
LAG = 1
WIDE = 8
DEPTH = 4
NARROW = 4
EARLY = 1


def kernel(
    a_hbm,
    cols_hbm,
    scales_hbm,
    counts_hbm,
    b_hbm,
    b_scales_hbm,
    keep_hbm,
    perm_hbm,
    out,
    cols,
    scales,
    counts,
    b_scales,
    keep,
    perm,
    table_sem,
    a_own,
    left,
    right,
    carry,
    result,
    total,
    load_sem,
    b_recv,
    b_up,
    b_down,
    b_cross,
    k_recv,
    k_down,
    k_mate,
    a_recv,
    a_mate,
    a_far,
    r_send,
    r_recv,
):
    w = lax.axis_index("wide")
    n = lax.axis_index("narrow")
    x = w % 2
    z = w // 2
    y = n // 2
    core = n % 2
    rows, share, slots, side = a_own.shape[:4]
    kb = b_hbm.shape[0] // side
    width = b_hbm.shape[1]
    across = w + 1 - 2 * x
    mate = n + 1 - 2 * core
    far = (n + 2) % 4
    diagonal = 3 - n

    barrier = pltpu.get_barrier_semaphore()
    for peer in ((w, mate), (w, far), (w, diagonal), (across, n)):
        pl.semaphore_signal(barrier, inc=1, device_id=peer, device_id_type=MESH)

    @pl.when(z > 0)
    def _():
        pl.semaphore_signal(barrier, inc=1, device_id=(w - 2, n), device_id_type=MESH)

    @pl.when(z < DEPTH - 1)
    def _():
        pl.semaphore_signal(barrier, inc=1, device_id=(w + 2, n), device_id_type=MESH)

    @pl.when((z == DEPTH - 2) & (core == 1))
    def _():
        pl.semaphore_signal(barrier, inc=1, device_id=(w + 2, mate), device_id_type=MESH)

    @pl.when((z == 0) & (core == 0))
    def _():
        pl.semaphore_signal(barrier, inc=1, device_id=(across, mate), device_id_type=MESH)

    tables = [
        pltpu.make_async_copy(source, kept, table_sem.at[i])
        for i, (source, kept) in enumerate(
            (
                (perm_hbm, perm),
                (cols_hbm, cols),
                (scales_hbm, scales),
                (counts_hbm, counts),
                (b_scales_hbm, b_scales),
                (keep_hbm, keep),
            )
        )
    ]
    for copy in tables:
        copy.start()
    load_a = pltpu.make_async_copy(a_hbm, a_own, load_sem.at[0])
    load_a.start()
    load_b = [
        pltpu.make_async_copy(
            b_hbm.at[t % kb * side : (t % kb + 1) * side, t // kb * side : (t // kb + 1) * side],
            right.at[w * PARTS + t],
            load_sem.at[1 + t],
        )
        for t in range(PARTS)
    ]
    for copy in load_b:
        copy.start()

    def piece(slot, sent, target):
        return pltpu.make_async_remote_copy(
            src_ref=right.at[slot],
            dst_ref=right.at[slot],
            send_sem=sent.at[0],
            recv_sem=b_recv.at[slot],
            device_id=(target, n),
            device_id_type=MESH,
        )

    def upward(slot):
        return piece(slot, b_up, w + 2)

    def downward(slot):
        return piece(slot, b_down, w - 2)

    def crossing(slot):
        return piece(slot, b_cross, across)

    def top_slot(t):
        return (2 * (DEPTH - 1) + x) * PARTS + t

    def lift(t, source, target, sent, landed, wide, narrow):
        return pltpu.make_async_remote_copy(
            src_ref=source,
            dst_ref=target,
            send_sem=sent,
            recv_sem=landed,
            device_id=(wide, narrow),
            device_id_type=MESH,
        )

    def enter(t):
        slot = w * PARTS + t
        return lift(t, right.at[slot], carry.at[t], b_down.at[0], k_recv.at[t], w - 2, mate)

    def carry_down(t):
        return lift(t, carry.at[t], carry.at[t], k_down.at[0], k_recv.at[t], w - 2, n)

    def carry_mate(t):
        slot = top_slot(t)
        return lift(t, carry.at[t], right.at[slot], k_mate.at[0], b_recv.at[slot], w, mate)

    def carry_cross(t):
        slot = top_slot(t)
        return lift(t, carry.at[t], right.at[slot], k_down.at[0], b_recv.at[slot], across, mate)

    def block(origin, pair, j, sent, target):
        return pltpu.make_async_remote_copy(
            src_ref=left.at[origin, pair, j],
            dst_ref=left.at[origin, pair, j],
            send_sem=sent,
            recv_sem=a_recv.at[origin, pair, j],
            device_id=(w, target),
            device_id_type=MESH,
        )

    def to_far(pair, j):
        return block(n, pair, j, a_far.at[0], far)

    def to_mate(pair, j):
        return block(n, pair, j, a_mate.at[0], mate)

    def from_far(pair, j):
        return block(far, pair, j, a_far.at[0], far)

    def pass_on(pair, j):
        return block(far, pair, j, a_mate.at[1], mate)

    def home(q):
        found = jnp.int32(0)
        for r in range(rows):
            found = jnp.where(perm[0, r] == q, r, found)
        return found

    def scale(pair, j):
        s = n * share + j
        panel = (w - s + WIDE) % WIDE
        for c in range(2):
            r = home(2 * pair + c)
            weights, places = [], []
            for m in range(slots):
                place = cols[r, m, s]
                live = jnp.where(m < counts[r, s], 1.0, 0.0)
                weights.append(scales[r, m, s] * b_scales[panel * kb + place] * live)
                places.append(place)
            for k in range(kb):
                value = None
                for m in range(slots):
                    weight = jnp.where(places[m] == k, weights[m], 0.0)
                    term = a_own[r, j, m].astype(jnp.float32) * weight
                    value = term if value is None else value + term
                left[n, pair, j, c * side : (c + 1) * side, k * side : (k + 1) * side] = (
                    value.astype(jnp.bfloat16)
                )

    pairs = (y, 1 - y)
    units = [(pair, j) for pair in pairs for j in range(share)]
    for copy in tables:
        copy.wait()
    load_a.wait()
    for unit in units[:EARLY]:
        scale(*unit)
    for copy in load_b:
        copy.wait()

    neighbours = jnp.where(z > 0, 1, 0) + jnp.where(z < DEPTH - 1, 1, 0)
    lifted = ((z == DEPTH - 1) & (core == 0)) | ((z == 0) & (core == 1))
    pl.semaphore_wait(barrier, 4 + neighbours + jnp.where(lifted, 1, 0))

    @pl.when((z == DEPTH - 1) & (core == 0))
    def _():
        for t in range(PARTS):
            enter(t).start()

    @pl.when((z == DEPTH - 1) & (core == 1))
    def _():
        for t in range(PARTS):
            downward(w * PARTS + t).start()

    for unit in units[:EARLY]:
        to_far(*unit).start()
    for t in range(PARTS):
        own = w * PARTS + t

        @pl.when(z < DEPTH - 1)
        def _():
            upward(own).start()

        @pl.when((z > 0) & (z < DEPTH - 1))
        def _():
            downward(own).start()

        crossing(own).start()

    for unit in units[:EARLY]:
        to_mate(*unit).start()
    for unit in units[EARLY:]:
        scale(*unit)
        to_far(*unit).start()
        to_mate(*unit).start()

    def relay(step, t):
        from_below = (w - 2 * step) * PARTS + t
        from_above = (w + 2 * step) * PARTS + t

        @pl.when(z - step >= 0)
        def _():
            upward(from_below).wait_recv()

            @pl.when(z < DEPTH - 1)
            def _():
                upward(from_below).start()

            crossing(from_below).start()

        @pl.when(z + step < DEPTH)
        def _():
            downward(from_above).wait_recv()

            @pl.when((z > 0) & ((z + step < DEPTH - 1) | (core == 1)))
            def _():
                downward(from_above).start()

            @pl.when((z > 0) | (step < DEPTH - 1) | (core == 1))
            def _():
                crossing(from_above).start()

    def ferry(step, t):
        @pl.when((z + step == DEPTH - 1) & (core == 1))
        def _():
            carry_down(t).wait_recv()
            if step < DEPTH - 1:
                carry_down(t).start()
            else:
                carry_cross(t).start()
            carry_mate(t).start()

    def hand_over(pair, j):
        from_far(pair, j).wait_recv()
        pass_on(pair, j).start()

    def mate_arrived(pair, j):
        block(mate, pair, j, a_mate.at[0], mate).wait_recv()

    def diagonal_arrived(pair, j):
        block(diagonal, pair, j, a_mate.at[1], mate).wait_recv()

    near = (
        z,
        jnp.where(z == 0, 1, z - 1),
        jnp.where(z == 0, 2, jnp.where(z == 3, 1, z + 1)),
        jnp.where(z < 2, 3, 0),
    )

    def peer_arrived(level, h):
        for t in range(h * kb, h * kb + kb):
            crossing((2 * level + 1 - x) * PARTS + t).wait_recv()

    def half(panel, h):
        return right[pl.ds(panel * PARTS + h * kb, kb)].reshape(kb * side, side)

    def term(pair, j, level, h):
        panel = 2 * level + (x if j == 0 else 1 - x)
        origin = ((w - panel + WIDE) % WIDE) // share
        if h is None:
            tile = jnp.concatenate([half(panel, i) for i in range(HALVES)], axis=1)
        else:
            tile = half(panel, h)
        return jnp.dot(left[origin, pair, j], tile, preferred_element_type=jnp.float32)

    def add(slot, pair, terms, first=False):
        value = None
        for j, level in terms:
            product = term(pair, j, near[level], None)
            value = product if value is None else value + product
        total[slot] = value if first else total[slot] + value

    give, hold = 1 - y, y

    def deliver(c, h, source, target):
        start = pl.multiple_of(n * width + h * side, side)
        return pltpu.make_async_remote_copy(
            src_ref=result.at[source, c, h],
            dst_ref=out.at[:, pl.ds(start, side)],
            send_sem=r_send.at[source],
            recv_sem=r_recv.at[n],
            device_id=(w, target),
            device_id_type=MESH,
        )

    for t in range(PARTS):
        relay(1, t)
        if t >= LAG:
            ferry(1, t - LAG)
    for t in range(PARTS - LAG, PARTS):
        ferry(1, t)
    hand_over(give, 0)
    for t in range(PARTS):
        ferry(2, t)
        relay(2, t)
        if t == 1:
            hand_over(give, 1)
    mate_arrived(give, 0)
    mate_arrived(give, 1)
    diagonal_arrived(give, 0)
    add(0, give, [(0, 0), (0, 1), (0, 2)], first=True)
    for t in range(PARTS // 2):
        ferry(3, t)
        relay(3, t)
    diagonal_arrived(give, 1)
    for level in range(2):
        for h in range(HALVES):
            peer_arrived(near[level], h)
    add(0, give, [(1, 0), (1, 1)])
    hand_over(hold, 0)
    for t in range(PARTS // 2, PARTS):
        ferry(3, t)
        relay(3, t)
    for h in range(HALVES):
        peer_arrived(near[2], h)
        value = total[0, :, h * side : (h + 1) * side] + term(give, 0, near[3], h)
        value = value + term(give, 1, near[2], h)
        peer_arrived(near[3], h)
        value = value + term(give, 1, near[3], h)
        for c in range(2):
            q = 2 * give + c
            kept = value[c * side : (c + 1) * side] * keep[h, home(q)].astype(jnp.float32)
            result[0, c, h] = kept.astype(jnp.bfloat16)
            deliver(c, h, 0, q).start()
    hand_over(hold, 1)
    mate_arrived(hold, 0)
    mate_arrived(hold, 1)
    diagonal_arrived(hold, 0)
    add(1, hold, [(0, 0), (0, 1), (0, 2), (0, 3)], first=True)
    diagonal_arrived(hold, 1)
    add(1, hold, [(1, 0), (1, 1), (1, 2), (1, 3)])
    for h in range(HALVES):
        c = 1 - core
        kept = total[1, pl.ds(pl.multiple_of(c * side, side), side), h * side : (h + 1) * side]
        result[1, 0, h] = (kept * keep[h, home(mate)].astype(jnp.float32)).astype(jnp.bfloat16)
        deliver(0, h, 1, mate).start()
    for h in range(HALVES):
        kept = total[1, pl.ds(pl.multiple_of(core * side, side), side), h * side : (h + 1) * side]
        start = pl.multiple_of(n * width + h * side, side)
        out[:, pl.ds(start, side)] = (kept * keep[h, home(n)].astype(jnp.float32)).astype(
            jnp.bfloat16
        )

    def drain(source, sem):
        pltpu.make_async_remote_copy(
            src_ref=source,
            dst_ref=source,
            send_sem=sem,
            recv_sem=b_recv.at[0],
            device_id=(w, mate),
            device_id_type=MESH,
        ).wait_send()

    for sem in (a_far.at[0], a_mate.at[0], a_mate.at[1]):
        drain(left.at[n], sem)
    for k in range(DEPTH):
        for c in range(2):

            @pl.when((z == k) & (core == c))
            def _(k=k, c=c):
                if k < DEPTH - 1:
                    drain(right.at[pl.ds(0, PARTS * (k + 1))], b_up.at[0])
                if k > 0:
                    levels = DEPTH - k if c == 1 else max(DEPTH - 1 - k, 1)
                    drain(right.at[pl.ds(0, PARTS * levels)], b_down.at[0])
                levels = DEPTH if c == 1 or k > 0 else DEPTH - 1
                drain(right.at[pl.ds(0, PARTS * levels)], b_cross.at[0])
                if c == 1 and k < DEPTH - 1:
                    drain(right.at[pl.ds(0, PARTS)], k_down.at[0])
                    drain(right.at[pl.ds(0, PARTS)], k_mate.at[0])

    drain(result.at[0], r_send.at[0])
    drain(result.at[1, 0], r_send.at[1])
    for origin in (mate, far, diagonal):
        place = out.at[:, pl.ds(pl.multiple_of(origin * width, width), width)]
        pltpu.make_async_remote_copy(
            src_ref=place,
            dst_ref=place,
            send_sem=r_send.at[0],
            recv_sem=r_recv.at[origin],
            device_id=(w, origin),
            device_id_type=MESH,
        ).wait_recv()


def fused(a_blocks, a_cols, a_scales, a_counts, b_panel, b_scales, keep_mask, row_perm):
    rows, share, slots, side = a_blocks.shape[:4]
    depth, width = b_panel.shape
    pieces = WIDE * PARTS
    in_place = pl.BlockSpec(memory_space=pltpu.HBM)
    dma = pltpu.SemaphoreType.DMA
    return pl.pallas_call(
        kernel,
        out_shape=pltpu.VMEM((side, width * NARROW), jnp.bfloat16),
        in_specs=[in_place] * 8,
        out_specs=pl.BlockSpec(memory_space=pltpu.VMEM),
        scratch_shapes=[
            pltpu.SMEM((rows, slots, a_cols.shape[1]), jnp.int32),
            pltpu.SMEM((rows, slots, a_cols.shape[1]), jnp.float32),
            pltpu.SMEM(a_counts.shape, jnp.int32),
            pltpu.SMEM(b_scales.shape, jnp.float32),
            pltpu.SMEM((keep_mask.shape[1], rows), jnp.int32),
            pltpu.SMEM(row_perm.shape, jnp.int32),
            dma((6,)),
            pltpu.VMEM(a_blocks.shape, jnp.bfloat16),
            pltpu.VMEM((NARROW, 2, share, 2 * side, depth), jnp.bfloat16),
            pltpu.VMEM((pieces, side, side), jnp.bfloat16),
            pltpu.VMEM((PARTS, side, side), jnp.bfloat16),
            pltpu.VMEM((2, 2, HALVES, side, side), jnp.bfloat16),
            pltpu.VMEM((2, 2 * side, width), jnp.float32),
            dma((1 + PARTS,)),
            dma((pieces,)),
            dma((1,)),
            dma((1,)),
            dma((1,)),
            dma((PARTS,)),
            dma((1,)),
            dma((1,)),
            dma((NARROW, 2, share)),
            dma((2,)),
            dma((1,)),
            dma((2,)),
            dma((NARROW,)),
        ],
        compiler_params=pltpu.CompilerParams(
            collective_id=0, has_side_effects=True, vmem_limit_bytes=60 * 2**20
        ),
    )(
        a_blocks,
        jnp.transpose(a_cols, (0, 2, 1)),
        jnp.transpose(a_scales, (0, 2, 1)),
        a_counts,
        b_panel,
        b_scales,
        jnp.transpose(keep_mask),
        row_perm,
    )


def shifted(block, axis, distance):
    devices = range(lax.axis_size(axis))
    route = [((i - distance) % len(devices), i) for i in devices]
    return lax.ppermute(block, axis, route)


def chosen(table, index):
    tail = (1,) * (table.ndim - 1)
    index = index.reshape(index.shape + tail)
    found = jnp.broadcast_to(table[0], index.shape[: index.ndim - len(tail)] + table.shape[1:])
    for k in range(1, table.shape[0]):
        found = jnp.where(index == k, table[k], found)
    return found


def section_term(row_blocks, slot_cols, weights, b_tiles):
    row_count = row_blocks.shape[0]
    slot_count = row_blocks.shape[1]
    block_side = row_blocks.shape[2]
    scaled = (row_blocks.astype(jnp.float32) * weights[:, :, None, None]).astype(jnp.bfloat16)
    left = jnp.transpose(scaled, (0, 2, 1, 3)).reshape(
        row_count, block_side, slot_count * block_side
    )
    right = chosen(b_tiles, slot_cols.reshape(-1)).reshape(
        row_count, slot_count * block_side, b_tiles.shape[2]
    )
    return jnp.einsum("rik,rkj->rij", left, right, preferred_element_type=jnp.float32)


def by_rings(a_blocks, a_cols, a_scales, a_counts, b_panel, b_scales, keep_mask, row_perm):
    wide_count = lax.axis_size("wide")
    narrow_count = lax.axis_size("narrow")
    device_row = lax.axis_index("wide")
    device_column = lax.axis_index("narrow")
    row_count, section_share, slot_count, block_side = a_blocks.shape[:4]
    section_total = section_share * narrow_count
    k_rows = b_panel.shape[0] // block_side
    out_width = b_panel.shape[1]
    col_blocks = out_width // block_side
    held = [a_blocks]
    for _ in range(narrow_count - 1):
        held.append(shifted(held[-1], "narrow", 1))
    held = jnp.stack(held)
    slot_ids = jnp.arange(slot_count, dtype=jnp.int32)
    accumulated = jnp.zeros((row_count, block_side, out_width), jnp.float32)
    current = b_panel.reshape(k_rows, block_side, out_width)
    for step_number in range(section_total):
        if step_number > 0:
            current = shifted(current, "wide", 1)
        back = (device_column - step_number // section_share) % narrow_count
        row_blocks = lax.dynamic_index_in_dim(held, back, keepdims=False)
        row_blocks = row_blocks[:, step_number % section_share]
        panel_number = (device_row - step_number) % wide_count
        slot_cols = a_cols[:, step_number]
        live_slots = (slot_ids[None, :] < a_counts[:, step_number][:, None]).astype(jnp.float32)
        weights = (
            a_scales[:, step_number]
            * chosen(lax.dynamic_slice(b_scales, (panel_number * k_rows,), (k_rows,)), slot_cols)
            * live_slots
        )
        accumulated = accumulated + section_term(row_blocks, slot_cols, weights, current)
    masked = (
        accumulated.reshape(row_count, block_side, col_blocks, block_side)
        * keep_mask.astype(jnp.float32)[:, None, :, None]
    )
    filtered = masked.astype(jnp.bfloat16).reshape(row_count, block_side, out_width)
    new_order = row_perm[0]
    positions = jnp.arange(row_count, dtype=jnp.int32)
    matches = (new_order[None, :] == positions[:, None]).astype(jnp.int32)
    inverse = jnp.sum(positions[None, :] * matches, axis=1)
    reordered = chosen(filtered, inverse).reshape(row_count * block_side, out_width)
    return lax.all_to_all(reordered, "narrow", split_axis=0, concat_axis=1, tiled=True)


def per_device(*operands):
    wide_count = lax.axis_size("wide")
    narrow_count = lax.axis_size("narrow")
    rows, share, slots, side = operands[0].shape[:4]
    depth, width = operands[4].shape
    fits = rows == 4 and share == 2 and depth == width == 2 * side
    if fits and narrow_count == NARROW and wide_count == WIDE:
        return fused(*operands)
    return by_rings(*operands)


def solution(mesh):
    in_specs = (
        P("wide", "narrow", None, None, None),
        P("wide", None, None),
        P("wide", None, None),
        P("wide", None),
        P("wide", "narrow"),
        P(),
        P("wide", "narrow"),
        P("wide", None),
    )
    out_specs = P(("wide", "narrow"), None)
    return jax.shard_map(
        per_device, mesh=mesh, in_specs=in_specs, out_specs=out_specs, check_vma=False
    )
```

```python
import functools

import jax
import jax.numpy as jnp
from jax import lax
from jax.experimental import pallas as pl
from jax.experimental.pallas import tpu as pltpu
from jax.sharding import PartitionSpec as P

MESH = pl.DeviceIdType.MESH
HALVES = 2
PARTS = 4
LAG = 2
WIDE = 8
DEPTH = 4
NARROW = 4
EARLY = 1


def kernel(
    a_hbm,
    cols_hbm,
    scales_hbm,
    counts_hbm,
    b_hbm,
    b_scales_hbm,
    keep_hbm,
    perm_hbm,
    out,
    cols,
    scales,
    counts,
    b_scales,
    keep,
    perm,
    table_sem,
    a_own,
    left,
    right,
    carry,
    result,
    total,
    load_sem,
    b_recv,
    b_up,
    b_down,
    b_cross,
    k_recv,
    k_down,
    k_mate,
    a_recv,
    a_mate,
    a_far,
    r_send,
    r_recv,
):
    w = lax.axis_index("wide")
    n = lax.axis_index("narrow")
    x = w % 2
    z = w // 2
    y = n // 2
    core = n % 2
    rows, share, slots, side = a_own.shape[:4]
    kb = b_hbm.shape[0] // side
    width = b_hbm.shape[1]
    across = w + 1 - 2 * x
    mate = n + 1 - 2 * core
    far = (n + 2) % 4
    diagonal = 3 - n

    barrier = pltpu.get_barrier_semaphore()
    for peer in ((w, mate), (w, far), (w, diagonal), (across, n)):
        pl.semaphore_signal(barrier, inc=1, device_id=peer, device_id_type=MESH)

    @pl.when(z > 0)
    def _():
        pl.semaphore_signal(barrier, inc=1, device_id=(w - 2, n), device_id_type=MESH)

    @pl.when(z < DEPTH - 1)
    def _():
        pl.semaphore_signal(barrier, inc=1, device_id=(w + 2, n), device_id_type=MESH)

    @pl.when((z == DEPTH - 2) & (core == 1))
    def _():
        pl.semaphore_signal(barrier, inc=1, device_id=(w + 2, mate), device_id_type=MESH)

    @pl.when((z == 0) & (core == 0))
    def _():
        pl.semaphore_signal(barrier, inc=1, device_id=(across, mate), device_id_type=MESH)

    tables = [
        pltpu.make_async_copy(source, kept, table_sem.at[i])
        for i, (source, kept) in enumerate(
            (
                (perm_hbm, perm),
                (cols_hbm, cols),
                (scales_hbm, scales),
                (counts_hbm, counts),
                (b_scales_hbm, b_scales),
                (keep_hbm, keep),
            )
        )
    ]
    for copy in tables:
        copy.start()
    load_a = pltpu.make_async_copy(a_hbm, a_own, load_sem.at[0])
    load_a.start()
    load_b = [
        pltpu.make_async_copy(
            b_hbm.at[t % kb * side : (t % kb + 1) * side, t // kb * side : (t // kb + 1) * side],
            right.at[w * PARTS + t],
            load_sem.at[1 + t],
        )
        for t in range(PARTS)
    ]
    for copy in load_b:
        copy.start()

    def piece(slot, sent, target):
        return pltpu.make_async_remote_copy(
            src_ref=right.at[slot],
            dst_ref=right.at[slot],
            send_sem=sent.at[0],
            recv_sem=b_recv.at[slot],
            device_id=(target, n),
            device_id_type=MESH,
        )

    def upward(slot):
        return piece(slot, b_up, w + 2)

    def downward(slot):
        return piece(slot, b_down, w - 2)

    def crossing(slot):
        return piece(slot, b_cross, across)

    def top_slot(t):
        return (2 * (DEPTH - 1) + x) * PARTS + t

    def lift(t, source, target, sent, landed, wide, narrow):
        return pltpu.make_async_remote_copy(
            src_ref=source,
            dst_ref=target,
            send_sem=sent,
            recv_sem=landed,
            device_id=(wide, narrow),
            device_id_type=MESH,
        )

    def enter(t):
        slot = w * PARTS + t
        return lift(t, right.at[slot], carry.at[t], b_down.at[0], k_recv.at[t], w - 2, mate)

    def carry_down(t):
        return lift(t, carry.at[t], carry.at[t], k_down.at[0], k_recv.at[t], w - 2, n)

    def carry_mate(t):
        slot = top_slot(t)
        return lift(t, carry.at[t], right.at[slot], k_mate.at[0], b_recv.at[slot], w, mate)

    def carry_cross(t):
        slot = top_slot(t)
        return lift(t, carry.at[t], right.at[slot], k_down.at[0], b_recv.at[slot], across, mate)

    def block(origin, pair, j, sent, target):
        return pltpu.make_async_remote_copy(
            src_ref=left.at[origin, pair, j],
            dst_ref=left.at[origin, pair, j],
            send_sem=sent,
            recv_sem=a_recv.at[origin, pair, j],
            device_id=(w, target),
            device_id_type=MESH,
        )

    def to_far(pair, j):
        return block(n, pair, j, a_far.at[0], far)

    def to_mate(pair, j):
        return block(n, pair, j, a_mate.at[0], mate)

    def from_far(pair, j):
        return block(far, pair, j, a_far.at[0], far)

    def pass_on(pair, j):
        return block(far, pair, j, a_mate.at[1], mate)

    def home(q):
        found = jnp.int32(0)
        for r in range(rows):
            found = jnp.where(perm[0, r] == q, r, found)
        return found

    def scale(pair, j):
        s = n * share + j
        panel = (w - s + WIDE) % WIDE
        for c in range(2):
            r = home(2 * pair + c)
            weights, places = [], []
            for m in range(slots):
                place = cols[r, m, s]
                live = jnp.where(m < counts[r, s], 1.0, 0.0)
                weights.append(scales[r, m, s] * b_scales[panel * kb + place] * live)
                places.append(place)
            for k in range(kb):
                value = None
                for m in range(slots):
                    weight = jnp.where(places[m] == k, weights[m], 0.0)
                    term = a_own[r, j, m].astype(jnp.float32) * weight
                    value = term if value is None else value + term
                left[n, pair, j, c * side : (c + 1) * side, k * side : (k + 1) * side] = (
                    value.astype(jnp.bfloat16)
                )

    pairs = (y, 1 - y)
    units = [(pair, j) for pair in pairs for j in range(share)]
    for copy in tables:
        copy.wait()
    load_a.wait()
    for unit in units[:EARLY]:
        scale(*unit)
    for copy in load_b:
        copy.wait()

    neighbours = jnp.where(z > 0, 1, 0) + jnp.where(z < DEPTH - 1, 1, 0)
    lifted = ((z == DEPTH - 1) & (core == 0)) | ((z == 0) & (core == 1))
    pl.semaphore_wait(barrier, 4 + neighbours + jnp.where(lifted, 1, 0))

    @pl.when((z == DEPTH - 1) & (core == 0))
    def _():
        for t in range(PARTS):
            enter(t).start()

    @pl.when((z == DEPTH - 1) & (core == 1))
    def _():
        for t in range(PARTS):
            downward(w * PARTS + t).start()

    for unit in units[:EARLY]:
        to_far(*unit).start()
    for t in range(PARTS):
        own = w * PARTS + t

        @pl.when(z < DEPTH - 1)
        def _():
            upward(own).start()

        @pl.when((z > 0) & (z < DEPTH - 1))
        def _():
            downward(own).start()

        crossing(own).start()

    for unit in units[:EARLY]:
        to_mate(*unit).start()
    for unit in units[EARLY:]:
        scale(*unit)
        to_far(*unit).start()
        to_mate(*unit).start()

    def relay(step, t):
        from_below = (w - 2 * step) * PARTS + t
        from_above = (w + 2 * step) * PARTS + t

        @pl.when(z - step >= 0)
        def _():
            upward(from_below).wait_recv()

            @pl.when(z < DEPTH - 1)
            def _():
                upward(from_below).start()

            crossing(from_below).start()

        @pl.when(z + step < DEPTH)
        def _():
            downward(from_above).wait_recv()

            @pl.when((z > 0) & ((z + step < DEPTH - 1) | (core == 1)))
            def _():
                downward(from_above).start()

            @pl.when((z > 0) | (step < DEPTH - 1) | (core == 1))
            def _():
                crossing(from_above).start()

    def ferry(step, t):
        @pl.when((z + step == DEPTH - 1) & (core == 1))
        def _():
            carry_down(t).wait_recv()
            if step < DEPTH - 1:
                carry_down(t).start()
            else:
                carry_cross(t).start()
            carry_mate(t).start()

    def hand_over(pair, j):
        from_far(pair, j).wait_recv()
        pass_on(pair, j).start()

    def mate_arrived(pair, j):
        block(mate, pair, j, a_mate.at[0], mate).wait_recv()

    def diagonal_arrived(pair, j):
        block(diagonal, pair, j, a_mate.at[1], mate).wait_recv()

    near = (
        z,
        jnp.where(z == 0, 1, z - 1),
        jnp.where(z == 0, 2, jnp.where(z == 3, 1, z + 1)),
        jnp.where(z < 2, 3, 0),
    )

    def peer_arrived(level, h):
        for t in range(h * kb, h * kb + kb):
            crossing((2 * level + 1 - x) * PARTS + t).wait_recv()

    def half(panel, h):
        return right[pl.ds(panel * PARTS + h * kb, kb)].reshape(kb * side, side)

    def term(pair, j, level, h):
        panel = 2 * level + (x if j == 0 else 1 - x)
        origin = ((w - panel + WIDE) % WIDE) // share
        if h is None:
            tile = jnp.concatenate([half(panel, i) for i in range(HALVES)], axis=1)
        else:
            tile = half(panel, h)
        return jnp.dot(left[origin, pair, j], tile, preferred_element_type=jnp.float32)

    def add(slot, pair, terms, first=False):
        value = None
        for j, level in terms:
            product = term(pair, j, near[level], None)
            value = product if value is None else value + product
        total[slot] = value if first else total[slot] + value

    give, hold = 1 - y, y

    def deliver(c, h, source, target):
        start = pl.multiple_of(n * width + h * side, side)
        return pltpu.make_async_remote_copy(
            src_ref=result.at[source, c, h],
            dst_ref=out.at[:, pl.ds(start, side)],
            send_sem=r_send.at[source],
            recv_sem=r_recv.at[n],
            device_id=(w, target),
            device_id_type=MESH,
        )

    for t in range(PARTS):
        relay(1, t)
        if t >= LAG:
            ferry(1, t - LAG)
    for t in range(PARTS - LAG, PARTS):
        ferry(1, t)
    hand_over(give, 0)
    for t in range(PARTS):
        ferry(2, t)
        relay(2, t)
        if t == 1:
            hand_over(give, 1)
    mate_arrived(give, 0)
    mate_arrived(give, 1)
    diagonal_arrived(give, 0)
    add(0, give, [(0, 0), (0, 1), (0, 2)], first=True)
    for t in range(PARTS // 2):
        ferry(3, t)
        relay(3, t)
    diagonal_arrived(give, 1)
    for level in range(2):
        for h in range(HALVES):
            peer_arrived(near[level], h)
    add(0, give, [(1, 0), (1, 1)])
    hand_over(hold, 0)
    for t in range(PARTS // 2, PARTS):
        ferry(3, t)
        relay(3, t)
    for h in range(HALVES):
        peer_arrived(near[2], h)
        value = total[0, :, h * side : (h + 1) * side] + term(give, 0, near[3], h)
        value = value + term(give, 1, near[2], h)
        peer_arrived(near[3], h)
        value = value + term(give, 1, near[3], h)
        for c in range(2):
            q = 2 * give + c
            kept = value[c * side : (c + 1) * side] * keep[h, home(q)].astype(jnp.float32)
            result[0, c, h] = kept.astype(jnp.bfloat16)
            deliver(c, h, 0, q).start()
    hand_over(hold, 1)
    mate_arrived(hold, 0)
    mate_arrived(hold, 1)
    diagonal_arrived(hold, 0)
    add(1, hold, [(0, 0), (0, 1), (0, 2), (0, 3)], first=True)
    diagonal_arrived(hold, 1)
    add(1, hold, [(1, 0), (1, 1), (1, 2), (1, 3)])
    for h in range(HALVES):
        c = 1 - core
        kept = total[1, pl.ds(pl.multiple_of(c * side, side), side), h * side : (h + 1) * side]
        result[1, 0, h] = (kept * keep[h, home(mate)].astype(jnp.float32)).astype(jnp.bfloat16)
        deliver(0, h, 1, mate).start()
    for h in range(HALVES):
        kept = total[1, pl.ds(pl.multiple_of(core * side, side), side), h * side : (h + 1) * side]
        start = pl.multiple_of(n * width + h * side, side)
        out[:, pl.ds(start, side)] = (kept * keep[h, home(n)].astype(jnp.float32)).astype(
            jnp.bfloat16
        )

    def drain(source, sem):
        pltpu.make_async_remote_copy(
            src_ref=source,
            dst_ref=source,
            send_sem=sem,
            recv_sem=b_recv.at[0],
            device_id=(w, mate),
            device_id_type=MESH,
        ).wait_send()

    for sem in (a_far.at[0], a_mate.at[0], a_mate.at[1]):
        drain(left.at[n], sem)
    for k in range(DEPTH):
        for c in range(2):

            @pl.when((z == k) & (core == c))
            def _(k=k, c=c):
                if k < DEPTH - 1:
                    drain(right.at[pl.ds(0, PARTS * (k + 1))], b_up.at[0])
                if k > 0:
                    levels = DEPTH - k if c == 1 else max(DEPTH - 1 - k, 1)
                    drain(right.at[pl.ds(0, PARTS * levels)], b_down.at[0])
                levels = DEPTH if c == 1 or k > 0 else DEPTH - 1
                drain(right.at[pl.ds(0, PARTS * levels)], b_cross.at[0])
                if c == 1 and k < DEPTH - 1:
                    drain(right.at[pl.ds(0, PARTS)], k_down.at[0])
                    drain(right.at[pl.ds(0, PARTS)], k_mate.at[0])

    drain(result.at[0], r_send.at[0])
    drain(result.at[1, 0], r_send.at[1])
    for origin in (mate, far, diagonal):
        place = out.at[:, pl.ds(pl.multiple_of(origin * width, width), width)]
        pltpu.make_async_remote_copy(
            src_ref=place,
            dst_ref=place,
            send_sem=r_send.at[0],
            recv_sem=r_recv.at[origin],
            device_id=(w, origin),
            device_id_type=MESH,
        ).wait_recv()


def fused(a_blocks, a_cols, a_scales, a_counts, b_panel, b_scales, keep_mask, row_perm):
    rows, share, slots, side = a_blocks.shape[:4]
    depth, width = b_panel.shape
    pieces = WIDE * PARTS
    in_place = pl.BlockSpec(memory_space=pltpu.HBM)
    dma = pltpu.SemaphoreType.DMA
    return pl.pallas_call(
        kernel,
        out_shape=pltpu.VMEM((side, width * NARROW), jnp.bfloat16),
        in_specs=[in_place] * 8,
        out_specs=pl.BlockSpec(memory_space=pltpu.VMEM),
        scratch_shapes=[
            pltpu.SMEM((rows, slots, a_cols.shape[1]), jnp.int32),
            pltpu.SMEM((rows, slots, a_cols.shape[1]), jnp.float32),
            pltpu.SMEM(a_counts.shape, jnp.int32),
            pltpu.SMEM(b_scales.shape, jnp.float32),
            pltpu.SMEM((keep_mask.shape[1], rows), jnp.int32),
            pltpu.SMEM(row_perm.shape, jnp.int32),
            dma((6,)),
            pltpu.VMEM(a_blocks.shape, jnp.bfloat16),
            pltpu.VMEM((NARROW, 2, share, 2 * side, depth), jnp.bfloat16),
            pltpu.VMEM((pieces, side, side), jnp.bfloat16),
            pltpu.VMEM((PARTS, side, side), jnp.bfloat16),
            pltpu.VMEM((2, 2, HALVES, side, side), jnp.bfloat16),
            pltpu.VMEM((2, 2 * side, width), jnp.float32),
            dma((1 + PARTS,)),
            dma((pieces,)),
            dma((1,)),
            dma((1,)),
            dma((1,)),
            dma((PARTS,)),
            dma((1,)),
            dma((1,)),
            dma((NARROW, 2, share)),
            dma((2,)),
            dma((1,)),
            dma((2,)),
            dma((NARROW,)),
        ],
        compiler_params=pltpu.CompilerParams(
            collective_id=0, has_side_effects=True, vmem_limit_bytes=60 * 2**20
        ),
    )(
        a_blocks,
        jnp.transpose(a_cols, (0, 2, 1)),
        jnp.transpose(a_scales, (0, 2, 1)),
        a_counts,
        b_panel,
        b_scales,
        jnp.transpose(keep_mask),
        row_perm,
    )


def shifted(block, axis, distance):
    devices = range(lax.axis_size(axis))
    route = [((i - distance) % len(devices), i) for i in devices]
    return lax.ppermute(block, axis, route)


def chosen(table, index):
    tail = (1,) * (table.ndim - 1)
    index = index.reshape(index.shape + tail)
    found = jnp.broadcast_to(table[0], index.shape[: index.ndim - len(tail)] + table.shape[1:])
    for k in range(1, table.shape[0]):
        found = jnp.where(index == k, table[k], found)
    return found


def section_term(row_blocks, slot_cols, weights, b_tiles):
    row_count = row_blocks.shape[0]
    slot_count = row_blocks.shape[1]
    block_side = row_blocks.shape[2]
    scaled = (row_blocks.astype(jnp.float32) * weights[:, :, None, None]).astype(jnp.bfloat16)
    left = jnp.transpose(scaled, (0, 2, 1, 3)).reshape(
        row_count, block_side, slot_count * block_side
    )
    right = chosen(b_tiles, slot_cols.reshape(-1)).reshape(
        row_count, slot_count * block_side, b_tiles.shape[2]
    )
    return jnp.einsum("rik,rkj->rij", left, right, preferred_element_type=jnp.float32)


def by_rings(a_blocks, a_cols, a_scales, a_counts, b_panel, b_scales, keep_mask, row_perm):
    wide_count = lax.axis_size("wide")
    narrow_count = lax.axis_size("narrow")
    device_row = lax.axis_index("wide")
    device_column = lax.axis_index("narrow")
    row_count, section_share, slot_count, block_side = a_blocks.shape[:4]
    section_total = section_share * narrow_count
    k_rows = b_panel.shape[0] // block_side
    out_width = b_panel.shape[1]
    col_blocks = out_width // block_side
    held = [a_blocks]
    for _ in range(narrow_count - 1):
        held.append(shifted(held[-1], "narrow", 1))
    held = jnp.stack(held)
    slot_ids = jnp.arange(slot_count, dtype=jnp.int32)
    accumulated = jnp.zeros((row_count, block_side, out_width), jnp.float32)
    current = b_panel.reshape(k_rows, block_side, out_width)
    for step_number in range(section_total):
        if step_number > 0:
            current = shifted(current, "wide", 1)
        back = (device_column - step_number // section_share) % narrow_count
        row_blocks = lax.dynamic_index_in_dim(held, back, keepdims=False)
        row_blocks = row_blocks[:, step_number % section_share]
        panel_number = (device_row - step_number) % wide_count
        slot_cols = a_cols[:, step_number]
        live_slots = (slot_ids[None, :] < a_counts[:, step_number][:, None]).astype(jnp.float32)
        weights = (
            a_scales[:, step_number]
            * chosen(lax.dynamic_slice(b_scales, (panel_number * k_rows,), (k_rows,)), slot_cols)
            * live_slots
        )
        accumulated = accumulated + section_term(row_blocks, slot_cols, weights, current)
    masked = (
        accumulated.reshape(row_count, block_side, col_blocks, block_side)
        * keep_mask.astype(jnp.float32)[:, None, :, None]
    )
    filtered = masked.astype(jnp.bfloat16).reshape(row_count, block_side, out_width)
    new_order = row_perm[0]
    positions = jnp.arange(row_count, dtype=jnp.int32)
    matches = (new_order[None, :] == positions[:, None]).astype(jnp.int32)
    inverse = jnp.sum(positions[None, :] * matches, axis=1)
    reordered = chosen(filtered, inverse).reshape(row_count * block_side, out_width)
    return lax.all_to_all(reordered, "narrow", split_axis=0, concat_axis=1, tiled=True)


def per_device(*operands):
    wide_count = lax.axis_size("wide")
    narrow_count = lax.axis_size("narrow")
    rows, share, slots, side = operands[0].shape[:4]
    depth, width = operands[4].shape
    fits = rows == 4 and share == 2 and depth == width == 2 * side
    if fits and narrow_count == NARROW and wide_count == WIDE:
        return fused(*operands)
    return by_rings(*operands)


def solution(mesh):
    in_specs = (
        P("wide", "narrow", None, None, None),
        P("wide", None, None),
        P("wide", None, None),
        P("wide", None),
        P("wide", "narrow"),
        P(),
        P("wide", "narrow"),
        P("wide", None),
    )
    out_specs = P(("wide", "narrow"), None)
    return jax.shard_map(
        per_device, mesh=mesh, in_specs=in_specs, out_specs=out_specs, check_vma=False
    )
```
